32 devices in a mesh: dp: 8 (over y, x, core), seq: 4 (over z).
Axes of the slice: x: 2, y: 2, z: 4, core: 2. Of those that a mesh axis runs over, the one named last changes fastest.
Arguments:
- qkv_input: bfloat16 [4096, 3, 3072], P(('dp', 'seq')), may hold values from -40 to 40
- latents: bfloat16 [4096, 3072], P(('dp', 'seq')), may hold values from -0.29882812 to 0.29882812
- cotangent: bfloat16 [4096, 3072], P(('dp', 'seq')), may hold values from -6 to 6
- out_weight: bfloat16 [3072, 3072], P('seq', 'dp'), may hold values from -0.109375 to 0.109375
- gate_table: float32 [64, 3072], replicated, may hold values from -8 to 8
- timesteps: int32 [8, 3], P('dp'), may hold values from 0 to 63
- frames: int32 [8, 3], P('dp'), may hold values from 1 to 4, 8 in all within a row
Outputs:
- output: bfloat16 [4096, 3072], P(('dp', 'seq'))
- grad_qkv: bfloat16 [4096, 3, 3072], P(('dp', 'seq'))
- grad_weight: float32 [3072, 3072], P('seq', 'dp')
The draws below stay inside these ranges and needn't reach their ends.
Inputs may be any that keep to these rules, and one draw needn't show every extreme that they name: Each pack's 3 clips cover its 8 frames exactly; in every pack the longest clip has 4 frames.
All inputs are finite; a program needn't handle non-finite values.
Results may differ from the reference program's by a relative error of at most 0.019.
Values may be sent and summed in bfloat16 or wider, within the bound.
A program may use at most 192 MiB of HBM per device.

```python
import math
import jax
import jax.numpy as jnp
import numpy as np
from jax import lax

D = 3072
HD = 128
FRAME_TOK = 64
CLIPS = 3
NT = 64
PACK = 512
PACKF = 8
MOSTF = 4
GROUPS = 8
TOKENS = 4096
N_SEQ = 4


def draw_qkv_input(key, part):
    first = jax.random.fold_in(key, 0)
    return jnp.clip(jax.random.normal(first, (TOKENS, 3, D), jnp.float32), -6.0, 6.0).astype(jnp.bfloat16)


def touch_ends(entries, rng, low, largest):
    dims = entries.shape
    spot = [jax.random.randint(jax.random.fold_in(rng, axis), (), 0, dims[axis]) for axis in range(len(dims))]
    entries = entries.at[tuple(spot)].set(low)
    longest = dims.index(max(dims))
    spot[longest] = (spot[longest] + 1) % dims[longest]
    return entries.at[tuple(spot)].set(largest)


def levels(key, extent, shards, smallest, high):
    gain, own = 1.0, jax.random.fold_in(key, 6)
    for dim, shards_of in shards:
        draws = jnp.exp(jax.random.uniform(jax.random.fold_in(own, dim), (shards_of,), jnp.float32, smallest / len(shards), high / len(shards)))
        gain = gain * jnp.repeat(draws, extent[dim] // shards_of).reshape([-1 if axis == dim else 1 for axis in range(len(extent))])
    return gain


def split_up(count, total, reach, lean):
    loads = [(1 << 20) // math.isqrt(rank ** lean) + 1 for rank in range(2, count + 1)]
    surplus, holding = total - reach - (count - 1), [1] * (count - 1)
    while surplus > 0:
        movable = [i for i in range(count - 1) if holding[i] < reach]
        mass, remaining = sum([loads[i] for i in movable]), surplus
        for i in movable:
            extra = min(reach - holding[i], max(1, remaining * loads[i] // mass), surplus)
            holding[i] = holding[i] + extra
            surplus = surplus - extra
    return np.array([reach] + holding)


def uneven_parts(rng, count, total, limit, lean):
    if count == 2:
        one = jax.random.randint(rng, (), max(1, total - limit), min(limit, total - 1) + 1)
        return jnp.stack([one, total - one])
    sizes = jnp.asarray(split_up(count, total, limit, lean), jnp.int32)
    twos = (count - 1) // 2
    donor, taker = sizes[1:1 + 2 * twos:2], sizes[2:2 + 2 * twos:2]
    slack = jnp.minimum(donor - 1, limit - taker)
    moved = jax.random.randint(jax.random.fold_in(rng, 1), (twos,), 0, 1 << 20) % (slack + 1)
    sizes = sizes.at[1:1 + 2 * twos:2].set(donor - moved).at[2:2 + 2 * twos:2].set(taker + moved)
    return sizes[jax.random.permutation(jax.random.fold_in(rng, 2), count)]


def gaussian(own_key, dims, scale, limit, cuts=(), kind=jnp.bfloat16):
    values = scale * jax.random.normal(own_key, dims, jnp.float32)
    if cuts:
        values = values * levels(own_key, dims, cuts, -0.22, 0.18)
    return jnp.clip(values, -limit, limit).astype(kind)


def setup_inputs(seed: int = 0) -> dict:
    streams_of = jax.random.split(jax.random.key(seed), 8)
    qkv_input = draw_qkv_input(jax.random.fold_in(streams_of[7], 71), 0)
    latents = gaussian(streams_of[1], (TOKENS, D), 0.05, 0.29882812, ((0, 32),))
    cotangent = gaussian(streams_of[2], (TOKENS, D), 1.0, 6.0, ((0, 32),))
    out_weight = gaussian(streams_of[3], (D, D), D ** -0.5, 0.109375, ((0, 4), (1, 8)))
    gate_table = gaussian(streams_of[4], (NT, D), 2.0, 8.0, (), jnp.float32)
    timesteps = touch_ends(jax.random.randint(streams_of[5], (GROUPS, CLIPS), 0, NT), jax.random.fold_in(streams_of[5], 1), 0, NT - 1).astype(jnp.int32)
    frames = jax.vmap(lambda own: uneven_parts(own, CLIPS, PACKF, MOSTF, 2))(jax.random.split(streams_of[6], GROUPS)).reshape((GROUPS, CLIPS)).astype(jnp.int32)
    return {"qkv_input": qkv_input, "latents": latents, "cotangent": cotangent, "out_weight": out_weight, "gate_table": gate_table, "timesteps": timesteps, "frames": frames}


def clip_index(frame_row, start, count):
    ends = jnp.cumsum(frame_row) * FRAME_TOK
    places = start + jnp.arange(count, dtype=jnp.int32)
    return lax.optimization_barrier(jnp.sum((places[:, None] >= ends[None, :]).astype(jnp.int32), axis=1))

def token_gate(frame_row, step_row, table, start, count):
    bins = jnp.arange(table.shape[0], dtype=jnp.int32)
    pick = (step_row[:, None] == bins[None, :]).astype(jnp.float32)
    clip_rows = jnp.dot(pick, table, precision=lax.Precision.HIGHEST)
    which = clip_index(frame_row, start, count)
    member = (which[:, None] == jnp.arange(frame_row.shape[0], dtype=jnp.int32)[None, :]).astype(jnp.float32)
    return jnp.dot(member, clip_rows, precision=lax.Precision.HIGHEST)

def attend(query, keys, values, which):
    rows = query.shape[0]
    count = query.shape[1] // HD
    qf = query.reshape(rows, count, HD).astype(jnp.float32)
    kf = keys.reshape(rows, count, HD).astype(jnp.float32)
    vf = values.reshape(rows, count, HD).astype(jnp.float32)
    scores = jnp.einsum('qhd,khd->hqk', qf, kf) / jnp.sqrt(jnp.float32(HD))
    same = which[:, None] == which[None, :]
    scores = jnp.where(same[None], scores, jnp.float32(-1e+30))
    top = lax.optimization_barrier(jnp.max(scores, axis=-1, keepdims=True))
    expo = jnp.exp(scores - top)
    probs = expo / lax.optimization_barrier(jnp.sum(expo, axis=-1, keepdims=True))
    probs_b = probs.astype(jnp.bfloat16)
    mixed = jnp.einsum('hqk,khd->qhd', probs_b.astype(jnp.float32), vf)
    return mixed.reshape(rows, count * HD)

def reference(qkv_input, latents, cotangent, out_weight, gate_table, timesteps, frames):
    width = D // N_SEQ
    grouped = qkv_input.reshape(GROUPS, PACK, 3, D)
    lat_groups = latents.reshape(GROUPS, PACK, D)
    cot_groups = cotangent.reshape(GROUPS, PACK, D)

    def one_pack(total, items):
        qkv_g, lat_g, cot_g, frame_row, step_row = items
        which = clip_index(frame_row, 0, PACK)
        gate = token_gate(frame_row, step_row, gate_table, 0, PACK)
        attn_f, back = jax.vjp(lambda a, b, c: attend(a, b, c, which), qkv_g[:, 0], qkv_g[:, 1], qkv_g[:, 2])
        attn = attn_f.astype(jnp.bfloat16)
        proj = jnp.zeros((PACK, D), jnp.float32)
        for index in range(N_SEQ):
            part = jnp.dot(attn[:, index * width:(index + 1) * width], out_weight[index * width:(index + 1) * width], preferred_element_type=jnp.float32).astype(jnp.bfloat16)
            part = lax.optimization_barrier(part)
            proj = proj + part.astype(jnp.float32)
        output = (lat_g.astype(jnp.float32) + gate * proj).astype(jnp.bfloat16)
        dproj = (gate * cot_g.astype(jnp.float32)).astype(jnp.bfloat16)
        total = total + jnp.dot(attn.T, dproj, preferred_element_type=jnp.float32)
        dattn = jnp.dot(dproj, out_weight.T, preferred_element_type=jnp.float32).astype(jnp.bfloat16)
        dattn = lax.optimization_barrier(dattn)
        grad_q, grad_k, grad_v = back(dattn.astype(jnp.float32))
        return (total, (output, jnp.stack([grad_q, grad_k, grad_v], axis=1)))
    start = jnp.zeros((D, D), jnp.float32)
    total, (outputs, grads) = lax.scan(one_pack, start, (grouped, lat_groups, cot_groups, frames, timesteps))
    return (outputs.reshape(TOKENS, D), grads.reshape(TOKENS, 3, D), total)
```

```python
import functools

import jax
import jax.numpy as jnp
from jax import lax
from jax.experimental import pallas as pl
from jax.experimental.pallas import tpu as pltpu
from jax.sharding import PartitionSpec as P

HD = 128
FRAME_TOK = 64
QUERY_TILE = 256
MESH = pl.DeviceIdType.MESH
TRANSPOSED_RHS = (((1,), (1,)), ((), ()))
TRANSPOSED_LHS = (((0,), (0,)), ((), ()))


def dot(a, b, dims=(((1,), (0,)), ((), ()))):
    return lax.dot_general(a, b, dims, preferred_element_type=jnp.float32)


def greet(n, dp, me):
    barrier = pltpu.get_barrier_semaphore()
    for k in range(1, n):
        pl.semaphore_signal(barrier, inc=1, device_id=(dp, lax.rem(me + k, n)), device_id_type=MESH)
    pl.semaphore_wait(barrier, n - 1)


def clip_of(frames_ref, places):
    end = 0
    which = jnp.zeros_like(places)
    for c in range(frames_ref.shape[1] - 1):
        end = end + frames_ref[0, c] * FRAME_TOK
        which = which + (places >= end).astype(jnp.int32)
    return which


def gate_rows(table_ref, steps_ref, frames_ref, start, count):
    places = start + lax.broadcasted_iota(jnp.int32, (count, 1), 0)
    which = clip_of(frames_ref, places)
    gate = table_ref[pl.ds(steps_ref[0, 0], 1), :]
    for c in range(1, steps_ref.shape[1]):
        gate = jnp.where(which >= c, table_ref[pl.ds(steps_ref[0, c], 1), :], gate)
    return gate


def probabilities(q, k, frames_ref, start, rows):
    count = q.shape[0]
    scores = dot(q, k, TRANSPOSED_RHS) * jnp.float32(HD ** -0.5)
    mine = clip_of(frames_ref, start + lax.broadcasted_iota(jnp.int32, (count, 1), 0))
    theirs = clip_of(frames_ref, lax.broadcasted_iota(jnp.int32, (1, rows), 1))
    scores = jnp.where(mine == theirs, scores, jnp.float32(-1e30))
    expo = jnp.exp(scores - jnp.max(scores, axis=-1, keepdims=True))
    return expo * (1.0 / jnp.sum(expo, axis=-1, keepdims=True))


def gather_kernel(
    n, qkv_ref, cot_ref, table_ref, steps_ref, frames_ref,
    heads_ref, attn_ref, piece_ref, dw_ref,
    flipped, own_sem, qs_sem, qr_sem, gs_sem, gr_sem,
):
    me = lax.axis_index("seq")
    dp = lax.axis_index("dp")
    group, _, rows, _ = heads_ref.shape
    tok = rows // n
    wide = dw_ref.shape[1]
    tile = min(QUERY_TILE, rows)

    def slab(block):
        return pl.ds(pl.multiple_of(block * tok, tok), tok)

    def block_copy(side, block):
        to = me + 1 if side == 0 else me - 1
        return pltpu.make_async_remote_copy(
            src_ref=piece_ref.at[slab(block), :],
            dst_ref=piece_ref.at[slab(block), :],
            send_sem=gs_sem.at[side, block],
            recv_sem=gr_sem.at[side, block],
            device_id=(dp, to),
            device_id_type=MESH,
        )

    def head_copy(k, h):
        peer = lax.rem(me + k, n)
        return pltpu.make_async_remote_copy(
            src_ref=qkv_ref.at[peer * group + h],
            dst_ref=heads_ref.at[h, :, slab(me), :],
            send_sem=qs_sem.at[k - 1, h],
            recv_sem=qr_sem.at[k - 1, h],
            device_id=(dp, peer),
            device_id_type=MESH,
        )

    def head_landed(k, h):
        source = lax.rem(me + n - k, n)
        pltpu.make_async_remote_copy(
            src_ref=qkv_ref.at[h],
            dst_ref=heads_ref.at[h, :, slab(source), :],
            send_sem=qs_sem.at[k - 1, h],
            recv_sem=qr_sem.at[k - 1, h],
            device_id=(dp, source),
            device_id_type=MESH,
        ).wait_recv()

    greet(n, dp, me)
    own = pltpu.make_async_copy(
        qkv_ref.at[pl.ds(me * group, group)], heads_ref.at[:, :, slab(me), :], own_sem
    )
    own.start()

    @pl.loop(0, group)
    def _(h):
        for k in range(1, n):
            head_copy(k, h).start()

    gate = gate_rows(table_ref, steps_ref, frames_ref, me * tok, tok)
    piece_ref[slab(me), :] = (gate * cot_ref[...].astype(jnp.float32)).astype(jnp.bfloat16)

    @pl.when(me < n - 1)
    def _():
        block_copy(0, me).start()

    @pl.when(me > 0)
    def _():
        block_copy(1, me).start()

    own.wait()

    def forward(h):
        for k in range(1, n):
            head_landed(k, h)

        @pl.loop(0, rows // tile)
        def _(t):
            here = pl.ds(pl.multiple_of(t * tile, tile), tile)
            probs = probabilities(
                heads_ref[h, 0, here, :], heads_ref[h, 1], frames_ref, t * tile, rows
            )
            mixed = dot(probs.astype(jnp.bfloat16), heads_ref[h, 2])
            attn_ref[here, pl.ds(pl.multiple_of(h * HD, HD), HD)] = mixed.astype(jnp.bfloat16)

    for s in range(1, n):
        @pl.when(me - s >= 0)
        def _():
            block_copy(0, me - s).wait_recv()

            @pl.when(me < n - 1)
            def _():
                block_copy(0, me - s).start()

        @pl.when(me + s < n)
        def _():
            block_copy(1, me + s).wait_recv()

            @pl.when(me > 0)
            def _():
                block_copy(1, me + s).start()

        pl.loop((s - 1) * group // (n - 1), s * group // (n - 1))(forward)

    flipped[...] = attn_ref[...].T
    step = 512

    @pl.loop(0, wide // step)
    def _(c):
        cols = pl.ds(pl.multiple_of(c * step, step), step)
        dw_ref[:, cols] = dot(flipped[...], piece_ref[:, cols]).astype(jnp.bfloat16)

    @pl.loop(0, group)
    def _(h):
        for k in range(1, n):
            head_copy(k, h).wait_send()

    for s in range(0, n):
        @pl.when((me - s >= 0) & (me < n - 1))
        def _():
            block_copy(0, me - s).wait_send()

        @pl.when((me + s < n) & (me > 0))
        def _():
            block_copy(1, me + s).wait_send()


def scatter_kernel(
    n, heads_ref, attn_ref, piece_ref, w_ref, lat_ref, table_ref, steps_ref, frames_ref,
    out_ref, grads_ref,
    part, landed, dattn, gbuf, own_sem, ps_sem, pr_sem, hs_sem, hr_sem,
):
    me = lax.axis_index("seq")
    dp = lax.axis_index("dp")
    group, _, rows, _ = heads_ref.shape
    tok = rows // n
    wide = w_ref.shape[1]
    tile = min(QUERY_TILE, rows)

    def slab(block):
        return pl.ds(pl.multiple_of(block * tok, tok), tok)

    def sum_copy(side, block):
        to = me + 1 if side == 0 else me - 1
        return pltpu.make_async_remote_copy(
            src_ref=part.at[block],
            dst_ref=landed.at[side, block],
            send_sem=ps_sem.at[side, block],
            recv_sem=pr_sem.at[side, block],
            device_id=(dp, to),
            device_id_type=MESH,
        )

    def grad_copy(k, h):
        peer = lax.rem(me + k, n)
        return pltpu.make_async_remote_copy(
            src_ref=gbuf.at[h, :, slab(peer), :],
            dst_ref=grads_ref.at[me * group + h],
            send_sem=hs_sem.at[k - 1, h],
            recv_sem=hr_sem.at[k - 1, h],
            device_id=(dp, peer),
            device_id_type=MESH,
        )

    def grad_landed(k, h):
        source = lax.rem(me + n - k, n)
        pltpu.make_async_remote_copy(
            src_ref=gbuf.at[h, :, slab(source), :],
            dst_ref=grads_ref.at[source * group + h],
            send_sem=hs_sem.at[k - 1, h],
            recv_sem=hr_sem.at[k - 1, h],
            device_id=(dp, source),
            device_id_type=MESH,
        ).wait_recv()

    def own_copy(h):
        return pltpu.make_async_copy(
            gbuf.at[h, :, slab(me), :], grads_ref.at[me * group + h], own_sem.at[h]
        )

    greet(n, dp, me)
    step = 512

    def project(block):
        @pl.loop(0, wide // step)
        def _(c):
            cols = pl.ds(pl.multiple_of(c * step, step), step)
            part[block, :, cols] = dot(attn_ref[slab(block), :], w_ref[:, cols]).astype(
                jnp.bfloat16
            )

    def relay(side, block):
        sum_copy(side, block).wait_recv()

        @pl.loop(0, tok // 16)
        def _(r):
            here = pl.ds(pl.multiple_of(r * 16, 16), 16)
            part[block, here, :] = (
                part[block, here, :].astype(jnp.float32)
                + landed[side, block, here, :].astype(jnp.float32)
            ).astype(jnp.bfloat16)

        sum_copy(side, block).start()

    for s in range(n - 1, -1, -1):
        @pl.when(me + s < n)
        def _():
            project(me + s)
            if s > 0:
                @pl.when(me == 0)
                def _():
                    sum_copy(0, me + s).start()

        if s > 0:
            @pl.when(me - s >= 0)
            def _():
                project(me - s)

                @pl.when(me == n - 1)
                def _():
                    sum_copy(1, me - s).start()

    head_cols = 2 * HD if (group * HD) % (2 * HD) == 0 else HD
    for c in range(0, group * HD, head_cols):
        dattn[:, c:c + head_cols] = dot(
            piece_ref[...], w_ref[c:c + head_cols, :], TRANSPOSED_RHS
        ).astype(jnp.bfloat16)

    def backward(h):
        q_cols = pl.ds(pl.multiple_of(h * HD, HD), HD)
        grad_k = jnp.zeros((rows, HD), jnp.float32)
        grad_v = jnp.zeros((rows, HD), jnp.float32)
        for t in range(rows // tile):
            here = slice(t * tile, (t + 1) * tile)
            q, keys = heads_ref[h, 0, here, :], heads_ref[h, 1]
            probs = probabilities(q, keys, frames_ref, t * tile, rows)
            up = dattn[here, q_cols]
            dprobs = dot(up, heads_ref[h, 2], TRANSPOSED_RHS)
            dprobs = dprobs.astype(jnp.bfloat16).astype(jnp.float32)
            dscores = probs * (dprobs - jnp.sum(probs * dprobs, axis=-1, keepdims=True))
            dscores = (dscores * jnp.float32(HD ** -0.5)).astype(jnp.bfloat16)
            gbuf[h, 0, here, :] = dot(dscores, keys).astype(jnp.bfloat16)
            grad_k = grad_k + dot(dscores, q, TRANSPOSED_LHS)
            grad_v = grad_v + dot(probs.astype(jnp.bfloat16), up, TRANSPOSED_LHS)
        gbuf[h, 1] = grad_k.astype(jnp.bfloat16)
        gbuf[h, 2] = grad_v.astype(jnp.bfloat16)
        for k in range(1, n):
            grad_copy(k, h).start()
        own_copy(h).start()

    for s in range(1, n):
        pl.loop((s - 1) * group // (n - 1), s * group // (n - 1))(backward)

        @pl.when((n - s > me) & (me > 0))
        def _():
            relay(0, n - s)

        @pl.when((s - 1 < me) & (me < n - 1))
        def _():
            relay(1, s - 1)

    @pl.when(me > 0)
    def _():
        sum_copy(0, me).wait_recv()

    @pl.when(me == 0)
    def _():
        landed[0, 0] = jnp.zeros_like(landed[0, 0])

    @pl.when(me < n - 1)
    def _():
        sum_copy(1, me).wait_recv()

    @pl.when(me == n - 1)
    def _():
        landed[1, n - 1] = jnp.zeros_like(landed[1, n - 1])

    gate = gate_rows(table_ref, steps_ref, frames_ref, me * tok, tok)
    proj = (
        part[me].astype(jnp.float32)
        + landed[0, me].astype(jnp.float32)
        + landed[1, me].astype(jnp.float32)
    )
    out_ref[...] = (lat_ref[...].astype(jnp.float32) + gate * proj).astype(jnp.bfloat16)

    for s in range(1, n):
        @pl.when(me + s < n)
        def _():
            sum_copy(0, me + s).wait_send()

        @pl.when(me - s >= 0)
        def _():
            sum_copy(1, me - s).wait_send()

    @pl.loop(0, group)
    def _(h):
        own_copy(h).wait()
        for k in range(1, n):
            grad_landed(k, h)
            grad_copy(k, h).wait_send()


def body(qkv_input, latents, cotangent, out_weight, gate_table, timesteps, frames):
    tok, wide = latents.shape
    n = lax.axis_size("seq")
    rows = tok * n
    heads = wide // HD
    group = heads // n
    bf16 = jnp.bfloat16
    vmem = pl.BlockSpec(memory_space=pltpu.VMEM)
    smem = pl.BlockSpec(memory_space=pltpu.SMEM)
    anyspace = pl.BlockSpec(memory_space=pl.ANY)
    dma = pltpu.SemaphoreType.DMA

    w_rows = lax.all_gather(out_weight, "dp", axis=1, tiled=True)
    by_head = qkv_input.reshape(tok, 3, heads, HD).transpose(2, 1, 0, 3)
    flops = 2 * rows * wide * group * HD
    packed, attn, piece, d_weight = pl.pallas_call(
        functools.partial(gather_kernel, n),
        out_shape=(
            jax.ShapeDtypeStruct((group, 3, rows, HD), bf16),
            jax.ShapeDtypeStruct((rows, group * HD), bf16),
            jax.ShapeDtypeStruct((rows, wide), bf16),
            jax.ShapeDtypeStruct((group * HD, wide), bf16),
        ),
        in_specs=[anyspace, vmem, vmem, smem, smem],
        out_specs=(vmem, vmem, vmem, vmem),
        scratch_shapes=[
            pltpu.VMEM((group * HD, rows), bf16),
            dma,
            dma((n - 1, group)),
            dma((n - 1, group)),
            dma((2, n)),
            dma((2, n)),
        ],
        compiler_params=pltpu.CompilerParams(
            collective_id=0, has_side_effects=True, vmem_limit_bytes=40 * 2**20
        ),
        cost_estimate=pl.CostEstimate(
            flops=20 * flops, bytes_accessed=200 * 2**20, transcendentals=0
        ),
        name="gather_and_attend",
    )(by_head, cotangent, gate_table, timesteps, frames)

    grad_weight = lax.psum_scatter(d_weight, "dp", scatter_dimension=1, tiled=True)

    output, grads = pl.pallas_call(
        functools.partial(scatter_kernel, n),
        out_shape=(
            jax.ShapeDtypeStruct((tok, wide), bf16),
            jax.ShapeDtypeStruct((heads, 3, tok, HD), bf16),
        ),
        in_specs=[vmem, vmem, vmem, vmem, vmem, vmem, smem, smem],
        out_specs=(vmem, anyspace),
        scratch_shapes=[
            pltpu.VMEM((n, tok, wide), bf16),
            pltpu.VMEM((2, n, tok, wide), bf16),
            pltpu.VMEM((rows, group * HD), bf16),
            pltpu.VMEM((group, 3, rows, HD), bf16),
            dma((group,)),
            dma((2, n)),
            dma((2, n)),
            dma((n - 1, group)),
            dma((n - 1, group)),
        ],
        compiler_params=pltpu.CompilerParams(
            collective_id=1, has_side_effects=True, vmem_limit_bytes=56 * 2**20
        ),
        cost_estimate=pl.CostEstimate(
            flops=20 * flops, bytes_accessed=200 * 2**20, transcendentals=0
        ),
        name="project_and_scatter",
    )(packed, attn, piece, w_rows, latents, gate_table, timesteps, frames)

    grad_qkv = grads.transpose(2, 1, 0, 3).reshape(tok, 3, wide)
    return output, grad_qkv, grad_weight.astype(jnp.float32)


def solution(mesh):
    placed = (
        P(("dp", "seq"), None, None),
        P(("dp", "seq"), None),
        P(("dp", "seq"), None),
        P("seq", "dp"),
        P(),
        P("dp", None),
        P("dp", None),
    )
    return jax.shard_map(
        body,
        mesh=mesh,
        in_specs=placed,
        out_specs=(P(("dp", "seq"), None), P(("dp", "seq"), None, None), P("seq", "dp")),
        check_vma=False,
    )
```

```python
import functools

import jax
import jax.numpy as jnp
from jax import lax
from jax.experimental import pallas as pl
from jax.experimental.pallas import tpu as pltpu
from jax.sharding import PartitionSpec as P

HD = 128
FRAME_TOK = 64
QUERY_TILE = 256
MESH = pl.DeviceIdType.MESH
TRANSPOSED_RHS = (((1,), (1,)), ((), ()))
TRANSPOSED_LHS = (((0,), (0,)), ((), ()))


def dot(a, b, dims=(((1,), (0,)), ((), ()))):
    return lax.dot_general(a, b, dims, preferred_element_type=jnp.float32)


def greet(devices):
    barrier = pltpu.get_barrier_semaphore()
    for device in devices:
        pl.semaphore_signal(barrier, inc=1, device_id=device, device_id_type=MESH)
    pl.semaphore_wait(barrier, len(devices))


def clip_of(frames_ref, places):
    end = 0
    which = jnp.zeros_like(places)
    for c in range(frames_ref.shape[1] - 1):
        end = end + frames_ref[0, c] * FRAME_TOK
        which = which + (places >= end).astype(jnp.int32)
    return which


def gate_rows(table_ref, steps_ref, frames_ref, start, count):
    places = start + lax.broadcasted_iota(jnp.int32, (count, 1), 0)
    which = clip_of(frames_ref, places)
    gate = table_ref[pl.ds(steps_ref[0, 0], 1), :]
    for c in range(1, steps_ref.shape[1]):
        gate = jnp.where(which >= c, table_ref[pl.ds(steps_ref[0, c], 1), :], gate)
    return gate


def probabilities(q, k, frames_ref, start, rows):
    count = q.shape[0]
    scores = dot(q, k, TRANSPOSED_RHS) * jnp.float32(HD ** -0.5)
    mine = clip_of(frames_ref, start + lax.broadcasted_iota(jnp.int32, (count, 1), 0))
    theirs = clip_of(frames_ref, lax.broadcasted_iota(jnp.int32, (1, rows), 1))
    scores = jnp.where(mine == theirs, scores, jnp.float32(-1e30))
    expo = jnp.exp(scores - jnp.max(scores, axis=-1, keepdims=True))
    return expo * (1.0 / jnp.sum(expo, axis=-1, keepdims=True))


def sublayer_kernel(
    n, n_dp, stages,
    qkv_ref, lat_ref, cot_ref, wt_ref, table_ref, steps_ref, frames_ref,
    out_ref, grads_ref, gw_ref,
    heads, attn, piece, weight, dweight, sibling, chips, part, landed, dattn, gbuf,
    own_sem, keep_sem, wo_sem, qs_sem, qr_sem, gs_sem, gr_sem,
    ws_sem, wr_sem, fs_sem, fr_sem, ps_sem, pr_sem, hs_sem, hr_sem,
    ss_sem, sr_sem, cs_sem, cr_sem,
):
    me = lax.axis_index("seq")
    dp = lax.axis_index("dp")
    core = lax.rem(dp, 2)
    chip = lax.div(dp, 2)
    n_chips = n_dp // 2
    rows, span = attn.shape
    tok, wide = out_ref.shape
    cols = wt_ref.shape[0]
    tile = min(QUERY_TILE, rows)
    chunk = span // stages
    step = 512

    def slab(block):
        return pl.ds(pl.multiple_of(block * tok, tok), tok)

    def owned(block):
        return pl.ds(pl.multiple_of(block * cols, cols), cols)

    def lanes(start):
        return pl.ds(pl.multiple_of(start, HD), chunk)

    def remote(src, dst, send, recv, device):
        return pltpu.make_async_remote_copy(
            src_ref=src, dst_ref=dst, send_sem=send, recv_sem=recv,
            device_id=device, device_id_type=MESH,
        )

    twin = (dp + 1 - 2 * core, me)

    def along(k):
        return (dp, lax.rem(me + k, n))

    def across(k):
        return (2 * lax.rem(chip + k, n_chips) + core, me)

    def block_copy(side, block):
        here = piece.at[slab(block), :]
        to = lax.rem(me + 1, n) if side == 0 else lax.rem(me + n - 1, n)
        return remote(here, here, gs_sem.at[side, block], gr_sem.at[side, block], (dp, to))

    def head_copy(k, c, source):
        peer = along(k)
        return remote(
            qkv_ref.at[:, :, lanes(peer[1] * span + c * chunk)],
            heads.at[:, slab(source), lanes(c * chunk)],
            qs_sem.at[k - 1, c], qr_sem.at[k - 1, c], peer,
        )

    def weight_copy(k, source):
        return remote(
            wt_ref, weight.at[owned(2 * source + core), :],
            ws_sem.at[k - 1], wr_sem.at[k - 1], across(k),
        )

    def weight_pass(k, source, side):
        here = weight.at[owned(2 * source + side), :]
        return remote(here, here, fs_sem.at[k], fr_sem.at[k], twin)

    def sum_copy(side, block):
        to = lax.rem(me + 1, n) if side == 0 else lax.rem(me + n - 1, n)
        return remote(
            part.at[slab(block), :], landed.at[side, block],
            ps_sem.at[side, block], pr_sem.at[side, block], (dp, to),
        )

    def grad_copy(k, c, source):
        peer = along(k)
        return remote(
            gbuf.at[:, slab(peer[1]), lanes(c * chunk)],
            grads_ref.at[:, :, lanes(source * span + c * chunk)],
            hs_sem.at[k - 1, c], hr_sem.at[k - 1, c], peer,
        )

    def grad_keep(c):
        return pltpu.make_async_copy(
            gbuf.at[:, slab(me), lanes(c * chunk)],
            grads_ref.at[:, :, lanes(me * span + c * chunk)], keep_sem.at[c],
        )

    def pair_copy(q, side):
        return remote(
            dweight.at[owned(2 * q + side), :], sibling.at[q],
            ss_sem.at[q], sr_sem.at[q], twin,
        )

    def chip_copy(k):
        return remote(
            dweight.at[owned(2 * lax.rem(chip + k, n_chips) + core), :], chips.at[k - 1],
            cs_sem.at[k - 1], cr_sem.at[k - 1], across(k),
        )

    greet(
        [along(k) for k in range(1, n)] + [across(k) for k in range(1, n_chips)] + [twin]
    )

    gate = gate_rows(table_ref, steps_ref, frames_ref, me * tok, tok)
    piece[slab(me), :] = (gate * cot_ref[...].astype(jnp.float32)).astype(jnp.bfloat16)

    @pl.when(me < n - 1)
    def _():
        block_copy(0, me).start()

    @pl.when(me > 0)
    def _():
        block_copy(1, me).start()

    def send_heads(c):
        for k in range(1, n):
            head_copy(k, c, me).start()

    send_heads(0)
    for k in range(1, n_chips):
        weight_copy(k, chip).start()
    own_weight = pltpu.make_async_copy(wt_ref, weight.at[owned(dp), :], wo_sem)
    own_weight.start()
    own = pltpu.make_async_copy(
        qkv_ref.at[:, :, pl.ds(pl.multiple_of(me * span, span), span)],
        heads.at[:, slab(me), :], own_sem,
    )
    own.start()
    own_weight.wait()
    weight_pass(0, chip, core).start()
    own.wait()

    def forward(c):
        for k in range(1, n):
            head_copy(k, c, lax.rem(me + n - k, n)).wait_recv()

        @pl.loop(0, (chunk // HD) * (rows // tile))
        def _(i):
            t, h = lax.rem(i, rows // tile), lax.div(i, rows // tile)
            here = pl.ds(pl.multiple_of(t * tile, tile), tile)
            head = pl.ds(pl.multiple_of(c * chunk + h * HD, HD), HD)
            probs = probabilities(
                heads[0, here, head], heads[1, :, head], frames_ref, t * tile, rows
            )
            mixed = dot(probs.astype(jnp.bfloat16), heads[2, :, head])
            attn[here, head] = mixed.astype(jnp.bfloat16)

    def backward(c):
        @pl.loop(0, chunk // HD)
        def _(h):
            head = pl.ds(pl.multiple_of(c * chunk + h * HD, HD), HD)
            grad_k = jnp.zeros((rows, HD), jnp.float32)
            grad_v = jnp.zeros((rows, HD), jnp.float32)
            for t in range(rows // tile):
                here = slice(t * tile, (t + 1) * tile)
                q, keys = heads[0, here, head], heads[1, :, head]
                probs = probabilities(q, keys, frames_ref, t * tile, rows)
                up = dattn[here, head]
                dprobs = dot(up, heads[2, :, head], TRANSPOSED_RHS)
                dprobs = dprobs.astype(jnp.bfloat16).astype(jnp.float32)
                dscores = probs * (dprobs - jnp.sum(probs * dprobs, axis=-1, keepdims=True))
                dscores = (dscores * jnp.float32(HD ** -0.5)).astype(jnp.bfloat16)
                gbuf[0, here, head] = dot(dscores, keys).astype(jnp.bfloat16)
                grad_k = grad_k + dot(dscores, q, TRANSPOSED_LHS)
                grad_v = grad_v + dot(probs.astype(jnp.bfloat16), up, TRANSPOSED_LHS)
            gbuf[1, :, head] = grad_k.astype(jnp.bfloat16)
            gbuf[2, :, head] = grad_v.astype(jnp.bfloat16)

        for k in range(1, n):
            grad_copy(k, c, me).start()
        grad_keep(c).start()

    def gather_hop(s):
        @pl.when(me - s >= 0)
        def _():
            block_copy(0, me - s).wait_recv()

            @pl.when(me < n - 1)
            def _():
                block_copy(0, me - s).start()

        @pl.when(me + s < n)
        def _():
            block_copy(1, me + s).wait_recv()

            @pl.when(me > 0)
            def _():
                block_copy(1, me + s).start()

    for c in range(stages):
        for s in range(1 + c * (n - 1) // stages, 1 + (c + 1) * (n - 1) // stages):
            gather_hop(s)
        if c + 1 < stages:
            send_heads(c + 1)
            forward(c)
        if c == 0:
            for k in range(1, n_chips):
                source = lax.rem(chip + n_chips - k, n_chips)
                weight_copy(k, source).wait_recv()
                weight_pass(k, source, core).start()

    for k in range(n_chips):
        weight_pass(k, lax.rem(chip + n_chips - k, n_chips), 1 - core).wait_recv()

    pair = 2 * HD if span % (2 * HD) == 0 else HD
    for c in range(0, span, pair):
        dattn[:, c:c + pair] = dot(piece[...], weight[:, c:c + pair]).astype(jnp.bfloat16)
    backward(0)
    forward(stages - 1)

    @pl.loop(0, wide // step)
    def _(i):
        here = pl.ds(pl.multiple_of(i * step, step), step)
        part[:, here] = dot(attn[...], weight[here, :], TRANSPOSED_RHS).astype(jnp.bfloat16)

    for s in range(n - 1, 0, -1):
        @pl.when((me == 0) & (me + s < n))
        def _():
            sum_copy(0, me + s).start()

        @pl.when((me == n - 1) & (me - s >= 0))
        def _():
            sum_copy(1, me - s).start()

    @pl.loop(0, wide // step)
    def _(i):
        here = pl.ds(pl.multiple_of(i * step, step), step)
        dweight[here, :] = dot(piece[:, here], attn[...], TRANSPOSED_LHS).astype(jnp.bfloat16)

    for q in range(n_chips):
        pair_copy(q, 1 - core).start()

    def add_into(target, spot, other, count):
        @pl.loop(0, count // 16)
        def _(r):
            mine = pl.ds(pl.multiple_of(spot * count + r * 16, 16), 16)
            theirs = pl.ds(pl.multiple_of(r * 16, 16), 16)
            target[mine, :] = (
                target[mine, :].astype(jnp.float32) + other[theirs, :].astype(jnp.float32)
            ).astype(jnp.bfloat16)

    def relay(side, block):
        sum_copy(side, block).wait_recv()
        add_into(part, block, landed.at[side, block], tok)
        sum_copy(side, block).start()

    for c in range(1, stages + 1):
        if c < stages:
            backward(c)
        if c == 1:
            for k in range(1, n_chips):
                q = lax.rem(chip + k, n_chips)
                pair_copy(q, core).wait_recv()
                add_into(dweight, 2 * q + core, sibling.at[q], cols)
                chip_copy(k).start()
        for s in range(1 + (c - 1) * (n - 1) // stages, 1 + c * (n - 1) // stages):
            @pl.when((n - s > me) & (me > 0))
            def _():
                relay(0, n - s)

            @pl.when((s - 1 < me) & (me < n - 1))
            def _():
                relay(1, s - 1)

    pair_copy(chip, core).wait_recv()
    total = dweight[owned(dp), :].astype(jnp.float32) + sibling[chip].astype(jnp.float32)
    for k in range(1, n_chips):
        chip_copy(k).wait_recv()
        total = total + chips[k - 1].astype(jnp.float32)
    gw_ref[...] = total

    @pl.when(me > 0)
    def _():
        sum_copy(0, me).wait_recv()

    @pl.when(me == 0)
    def _():
        landed[0, 0] = jnp.zeros_like(landed[0, 0])

    @pl.when(me < n - 1)
    def _():
        sum_copy(1, me).wait_recv()

    @pl.when(me == n - 1)
    def _():
        landed[1, n - 1] = jnp.zeros_like(landed[1, n - 1])

    gate = gate_rows(table_ref, steps_ref, frames_ref, me * tok, tok)
    proj = (
        part[slab(me), :].astype(jnp.float32)
        + landed[0, me].astype(jnp.float32)
        + landed[1, me].astype(jnp.float32)
    )
    out_ref[...] = (lat_ref[...].astype(jnp.float32) + gate * proj).astype(jnp.bfloat16)

    for s in range(n):
        @pl.when((me - s >= 0) & (me < n - 1))
        def _():
            block_copy(0, me - s).wait_send()

        @pl.when((me + s < n) & (me > 0))
        def _():
            block_copy(1, me + s).wait_send()

        if s > 0:
            @pl.when(me + s < n)
            def _():
                sum_copy(0, me + s).wait_send()

            @pl.when(me - s >= 0)
            def _():
                sum_copy(1, me - s).wait_send()

    for k in range(1, n_chips):
        weight_copy(k, chip).wait_send()
        chip_copy(k).wait_send()
    for q in range(n_chips):
        weight_pass(q, lax.rem(chip + n_chips - q, n_chips), core).wait_send()
        pair_copy(q, 1 - core).wait_send()
    for c in range(stages):
        grad_keep(c).wait()
        for k in range(1, n):
            head_copy(k, c, me).wait_send()
            grad_copy(k, c, me).wait_send()
            grad_copy(k, c, lax.rem(me + n - k, n)).wait_recv()


def body(qkv_input, latents, cotangent, out_weight, gate_table, timesteps, frames):
    tok, wide = latents.shape
    n, n_dp = lax.axis_size("seq"), lax.axis_size("dp")
    rows = tok * n
    span, cols = out_weight.shape
    stages = 3
    n_chips = n_dp // 2
    bf16 = jnp.bfloat16
    vmem = pl.BlockSpec(memory_space=pltpu.VMEM)
    smem = pl.BlockSpec(memory_space=pltpu.SMEM)
    dma = pltpu.SemaphoreType.DMA
    output, grads, grad_weight = pl.pallas_call(
        functools.partial(sublayer_kernel, n, n_dp, stages),
        out_shape=(
            jax.ShapeDtypeStruct((tok, wide), bf16),
            jax.ShapeDtypeStruct((3, tok, wide), bf16),
            jax.ShapeDtypeStruct((cols, span), jnp.float32),
        ),
        in_specs=[vmem, vmem, vmem, vmem, vmem, smem, smem],
        out_specs=(vmem, vmem, vmem),
        scratch_shapes=[
            pltpu.VMEM((3, rows, span), bf16),
            pltpu.VMEM((rows, span), bf16),
            pltpu.VMEM((rows, wide), bf16),
            pltpu.VMEM((wide, span), bf16),
            pltpu.VMEM((wide, span), bf16),
            pltpu.VMEM((n_chips, cols, span), bf16),
            pltpu.VMEM((n_chips - 1, cols, span), bf16),
            pltpu.VMEM((rows, wide), bf16),
            pltpu.VMEM((2, n, tok, wide), bf16),
            pltpu.VMEM((rows, span), bf16),
            pltpu.VMEM((3, rows, span), bf16),
            dma,
            dma((stages,)),
            dma,
            dma((n - 1, stages)),
            dma((n - 1, stages)),
            dma((2, n)),
            dma((2, n)),
            dma((n_chips - 1,)),
            dma((n_chips - 1,)),
            dma((n_chips,)),
            dma((n_chips,)),
            dma((2, n)),
            dma((2, n)),
            dma((n - 1, stages)),
            dma((n - 1, stages)),
            dma((n_chips,)),
            dma((n_chips,)),
            dma((n_chips - 1,)),
            dma((n_chips - 1,)),
        ],
        compiler_params=pltpu.CompilerParams(
            collective_id=0, has_side_effects=True, vmem_limit_bytes=60 * 2**20
        ),
        cost_estimate=pl.CostEstimate(
            flops=30 * rows * wide * span, bytes_accessed=32 * 2**20, transcendentals=0
        ),
        name="sublayer",
    )(
        qkv_input.transpose(1, 0, 2), latents, cotangent, out_weight.T,
        gate_table, timesteps, frames,
    )
    return output, grads.transpose(1, 0, 2), grad_weight.T


def solution(mesh):
    placed = (
        P(("dp", "seq"), None, None),
        P(("dp", "seq"), None),
        P(("dp", "seq"), None),
        P("seq", "dp"),
        P(),
        P("dp", None),
        P("dp", None),
    )
    return jax.shard_map(
        body,
        mesh=mesh,
        in_specs=placed,
        out_specs=(P(("dp", "seq"), None), P(("dp", "seq"), None, None), P("seq", "dp")),
        check_vma=False,
    )
```

```python
import functools

import jax
import jax.numpy as jnp
from jax import lax
from jax.experimental import pallas as pl
from jax.experimental.pallas import tpu as pltpu
from jax.sharding import PartitionSpec as P

HD = 128
FRAME_TOK = 64
QUERY_TILE = 256
MESH = pl.DeviceIdType.MESH
TRANSPOSED_RHS = (((1,), (1,)), ((), ()))
TRANSPOSED_LHS = (((0,), (0,)), ((), ()))


def dot(a, b, dims=(((1,), (0,)), ((), ()))):
    return lax.dot_general(a, b, dims, preferred_element_type=jnp.float32)


def greet(devices):
    barrier = pltpu.get_barrier_semaphore()
    for device in devices:
        pl.semaphore_signal(barrier, inc=1, device_id=device, device_id_type=MESH)
    pl.semaphore_wait(barrier, len(devices))


def clip_of(frames_ref, places):
    end = 0
    which = jnp.zeros_like(places)
    for c in range(frames_ref.shape[1] - 1):
        end = end + frames_ref[0, c] * FRAME_TOK
        which = which + (places >= end).astype(jnp.int32)
    return which


def gate_rows(table_ref, steps_ref, frames_ref, start, count):
    places = start + lax.broadcasted_iota(jnp.int32, (count, 1), 0)
    which = clip_of(frames_ref, places)
    gate = table_ref[pl.ds(steps_ref[0, 0], 1), :]
    for c in range(1, steps_ref.shape[1]):
        gate = jnp.where(which >= c, table_ref[pl.ds(steps_ref[0, c], 1), :], gate)
    return gate


def probabilities(q, k, frames_ref, start, rows):
    count = q.shape[0]
    scores = dot(q, k, TRANSPOSED_RHS) * jnp.float32(HD ** -0.5)
    mine = clip_of(frames_ref, start + lax.broadcasted_iota(jnp.int32, (count, 1), 0))
    theirs = clip_of(frames_ref, lax.broadcasted_iota(jnp.int32, (1, rows), 1))
    scores = jnp.where(mine == theirs, scores, jnp.float32(-1e30))
    expo = jnp.exp(scores - jnp.max(scores, axis=-1, keepdims=True))
    return expo * (1.0 / jnp.sum(expo, axis=-1, keepdims=True))


def sublayer_kernel(
    n, n_dp, stages,
    qkv_ref, lat_ref, cot_ref, w_ref, table_ref, steps_ref, frames_ref,
    out_ref, grads_ref, gw_ref,
    heads, attn, piece, weight, dweight, sibling, chips, part, landed, dattn, gbuf,
    own_sem, keep_sem, qs_sem, qr_sem, gs_sem, gr_sem,
    ws_sem, wr_sem, fs_sem, fr_sem, ps_sem, pr_sem, hs_sem, hr_sem,
    ss_sem, sr_sem, cs_sem, cr_sem,
):
    me = lax.axis_index("seq")
    dp = lax.axis_index("dp")
    core = lax.rem(dp, 2)
    chip = lax.div(dp, 2)
    n_chips = n_dp // 2
    rows, span = attn.shape
    tok, wide = out_ref.shape
    cols = wide // n_dp
    tile = min(QUERY_TILE, rows)
    chunk = span // stages
    step = 512

    def slab(block):
        return pl.ds(pl.multiple_of(block * tok, tok), tok)

    def owned(block):
        return pl.ds(pl.multiple_of(block * cols, cols), cols)

    def lanes(start):
        return pl.ds(pl.multiple_of(start, HD), chunk)

    def remote(src, dst, send, recv, device):
        return pltpu.make_async_remote_copy(
            src_ref=src, dst_ref=dst, send_sem=send, recv_sem=recv,
            device_id=device, device_id_type=MESH,
        )

    twin = (dp + 1 - 2 * core, me)

    def along(k):
        return (dp, lax.rem(me + k, n))

    def across(k):
        return (2 * lax.rem(chip + k, n_chips) + core, me)

    def block_copy(side, block):
        here = piece.at[slab(block), :]
        to = lax.rem(me + 1, n) if side == 0 else lax.rem(me + n - 1, n)
        return remote(here, here, gs_sem.at[side, block], gr_sem.at[side, block], (dp, to))

    def head_copy(k, c, source):
        peer = along(k)
        return remote(
            qkv_ref.at[:, :, lanes(peer[1] * span + c * chunk)],
            heads.at[:, slab(source), lanes(c * chunk)],
            qs_sem.at[k - 1, c], qr_sem.at[k - 1, c], peer,
        )

    def weight_copy(k):
        here = weight.at[owned(dp), :]
        return remote(
            here, here, ws_sem.at[k - 1], wr_sem.at[k - 1], across(k),
        )

    def weight_pass(k, source, side):
        here = weight.at[owned(2 * source + side), :]
        return remote(here, here, fs_sem.at[k], fr_sem.at[k], twin)

    def sum_copy(side, block):
        to = lax.rem(me + 1, n) if side == 0 else lax.rem(me + n - 1, n)
        return remote(
            part.at[slab(block), :], landed.at[side, block],
            ps_sem.at[side, block], pr_sem.at[side, block], (dp, to),
        )

    def grad_copy(k, c, source):
        peer = along(k)
        return remote(
            gbuf.at[:, slab(peer[1]), lanes(c * chunk)],
            grads_ref.at[:, :, lanes(source * span + c * chunk)],
            hs_sem.at[k - 1, c], hr_sem.at[k - 1, c], peer,
        )

    def grad_keep(c):
        return pltpu.make_async_copy(
            gbuf.at[:, slab(me), lanes(c * chunk)],
            grads_ref.at[:, :, lanes(me * span + c * chunk)], keep_sem.at[c],
        )

    def pair_copy(q, side):
        return remote(
            dweight.at[owned(2 * q + side), :], sibling.at[q],
            ss_sem.at[q], sr_sem.at[q], twin,
        )

    def chip_copy(k):
        return remote(
            dweight.at[owned(2 * lax.rem(chip + k, n_chips) + core), :], chips.at[k - 1],
            cs_sem.at[k - 1], cr_sem.at[k - 1], across(k),
        )

    greet(
        [along(k) for k in range(1, n)] + [across(k) for k in range(1, n_chips)] + [twin]
    )

    def send_heads(c):
        for k in range(1, n):
            head_copy(k, c, me).start()

    for c in range(stages):
        send_heads(c)
    own = pltpu.make_async_copy(
        qkv_ref.at[:, :, pl.ds(pl.multiple_of(me * span, span), span)],
        heads.at[:, slab(me), :], own_sem,
    )
    own.start()
    weight[owned(dp), :] = w_ref[...].T if w_ref.shape[0] == span else w_ref[...]
    for k in range(1, n_chips):
        weight_copy(k).start()
    weight_pass(0, chip, core).start()
    gate = gate_rows(table_ref, steps_ref, frames_ref, me * tok, tok)
    piece[slab(me), :] = (gate * cot_ref[...].astype(jnp.float32)).astype(jnp.bfloat16)
    own.wait()

    def start_gather():
        @pl.when(me < n - 1)
        def _():
            block_copy(0, me).start()

        @pl.when(me > 0)
        def _():
            block_copy(1, me).start()

    def heads_landed(c):
        for k in range(1, n):
            head_copy(k, c, lax.rem(me + n - k, n)).wait_recv()

    def forward(c):
        @pl.loop(0, (chunk // HD) * (rows // tile))
        def _(i):
            t, h = lax.rem(i, rows // tile), lax.div(i, rows // tile)
            here = pl.ds(pl.multiple_of(t * tile, tile), tile)
            head = pl.ds(pl.multiple_of(c * chunk + h * HD, HD), HD)
            probs = probabilities(
                heads[0, here, head], heads[1, :, head], frames_ref, t * tile, rows
            )
            mixed = dot(probs.astype(jnp.bfloat16), heads[2, :, head])
            attn[here, head] = mixed.astype(jnp.bfloat16)

    def backward(c):
        @pl.loop(0, chunk // HD)
        def _(h):
            head = pl.ds(pl.multiple_of(c * chunk + h * HD, HD), HD)
            grad_k = jnp.zeros((rows, HD), jnp.float32)
            grad_v = jnp.zeros((rows, HD), jnp.float32)
            for t in range(rows // tile):
                here = slice(t * tile, (t + 1) * tile)
                q, keys = heads[0, here, head], heads[1, :, head]
                probs = probabilities(q, keys, frames_ref, t * tile, rows)
                up = dattn[here, head]
                dprobs = dot(up, heads[2, :, head], TRANSPOSED_RHS)
                dprobs = dprobs.astype(jnp.bfloat16).astype(jnp.float32)
                dscores = probs * (dprobs - jnp.sum(probs * dprobs, axis=-1, keepdims=True))
                dscores = (dscores * jnp.float32(HD ** -0.5)).astype(jnp.bfloat16)
                gbuf[0, here, head] = dot(dscores, keys).astype(jnp.bfloat16)
                grad_k = grad_k + dot(dscores, q, TRANSPOSED_LHS)
                grad_v = grad_v + dot(probs.astype(jnp.bfloat16), up, TRANSPOSED_LHS)
            gbuf[1, :, head] = grad_k.astype(jnp.bfloat16)
            gbuf[2, :, head] = grad_v.astype(jnp.bfloat16)

        for k in range(1, n):
            grad_copy(k, c, me).start()
        grad_keep(c).start()

    def gather_hop(s):
        @pl.when(me - s >= 0)
        def _():
            block_copy(0, me - s).wait_recv()

            @pl.when(me < n - 1)
            def _():
                block_copy(0, me - s).start()

        @pl.when(me + s < n)
        def _():
            block_copy(1, me + s).wait_recv()

            @pl.when(me > 0)
            def _():
                block_copy(1, me + s).start()

    heads_landed(0)
    start_gather()
    forward(0)
    for k in range(1, n_chips):
        source = lax.rem(chip + n_chips - k, n_chips)
        weight_copy(k).wait_recv()
        weight_pass(k, source, core).start()
    for c in range(1, stages):
        heads_landed(c)
        forward(c)
    for k in range(n_chips):
        weight_pass(k, lax.rem(chip + n_chips - k, n_chips), 1 - core).wait_recv()

    @pl.loop(0, wide // step)
    def _(i):
        here = pl.ds(pl.multiple_of(i * step, step), step)
        part[:, here] = dot(attn[...], weight[here, :], TRANSPOSED_RHS).astype(jnp.bfloat16)

    for s in range(n - 1, 0, -1):
        @pl.when((me == 0) & (me + s < n))
        def _():
            sum_copy(0, me + s).start()

        @pl.when((me == n - 1) & (me - s >= 0))
        def _():
            sum_copy(1, me - s).start()

    for s in range(1, n):
        gather_hop(s)

    pair = 2 * HD if span % (2 * HD) == 0 else HD
    for c in range(0, span, pair):
        dattn[:, c:c + pair] = dot(piece[...], weight[:, c:c + pair]).astype(jnp.bfloat16)

    def add_into(target, spot, other, count):
        @pl.loop(0, count // 16)
        def _(r):
            mine = pl.ds(pl.multiple_of(spot * count + r * 16, 16), 16)
            theirs = pl.ds(pl.multiple_of(r * 16, 16), 16)
            target[mine, :] = (
                target[mine, :].astype(jnp.float32) + other[theirs, :].astype(jnp.float32)
            ).astype(jnp.bfloat16)

    def relay(side, block):
        sum_copy(side, block).wait_recv()
        add_into(part, block, landed.at[side, block], tok)
        sum_copy(side, block).start()

    def relay_right(s):
        @pl.when((n - s > me) & (me > 0))
        def _():
            relay(0, n - s)

    def relay_left(s):
        @pl.when((s - 1 < me) & (me < n - 1))
        def _():
            relay(1, s - 1)

    for c in range(stages):
        backward(c)
        if c == 0:
            @pl.loop(0, wide // step)
            def _(i):
                here = pl.ds(pl.multiple_of(i * step, step), step)
                grown = dot(piece[:, here], attn[...], TRANSPOSED_LHS)
                dweight[here, :] = grown.astype(jnp.bfloat16)

            for q in range(n_chips):
                pair_copy(q, 1 - core).start()
        if c == 1:
            for k in range(1, n_chips):
                q = lax.rem(chip + k, n_chips)
                pair_copy(q, core).wait_recv()
                add_into(dweight, 2 * q + core, sibling.at[q], cols)
                chip_copy(k).start()
        for s in range(1 + c * (n - 1) // stages, 1 + (c + 1) * (n - 1) // stages):
            @pl.when(2 * me < n)
            def _():
                relay_right(s)
                relay_left(s)

            @pl.when(2 * me >= n)
            def _():
                relay_left(s)
                relay_right(s)

    pair_copy(chip, core).wait_recv()
    total = dweight[owned(dp), :].astype(jnp.float32) + sibling[chip].astype(jnp.float32)
    for k in range(1, n_chips):
        chip_copy(k).wait_recv()
        total = total + chips[k - 1].astype(jnp.float32)
    gw_ref[...] = total.T if gw_ref.shape[0] == span else total

    @pl.when(me > 0)
    def _():
        sum_copy(0, me).wait_recv()

    @pl.when(me == 0)
    def _():
        landed[0, 0] = jnp.zeros_like(landed[0, 0])

    @pl.when(me < n - 1)
    def _():
        sum_copy(1, me).wait_recv()

    @pl.when(me == n - 1)
    def _():
        landed[1, n - 1] = jnp.zeros_like(landed[1, n - 1])

    gate = gate_rows(table_ref, steps_ref, frames_ref, me * tok, tok)
    proj = (
        part[slab(me), :].astype(jnp.float32)
        + landed[0, me].astype(jnp.float32)
        + landed[1, me].astype(jnp.float32)
    )
    out_ref[...] = (lat_ref[...].astype(jnp.float32) + gate * proj).astype(jnp.bfloat16)

    for s in range(n):
        @pl.when((me - s >= 0) & (me < n - 1))
        def _():
            block_copy(0, me - s).wait_send()

        @pl.when((me + s < n) & (me > 0))
        def _():
            block_copy(1, me + s).wait_send()

        if s > 0:
            @pl.when(me + s < n)
            def _():
                sum_copy(0, me + s).wait_send()

            @pl.when(me - s >= 0)
            def _():
                sum_copy(1, me - s).wait_send()

    for k in range(1, n_chips):
        weight_copy(k).wait_send()
        chip_copy(k).wait_send()
    for q in range(n_chips):
        weight_pass(q, lax.rem(chip + n_chips - q, n_chips), core).wait_send()
        pair_copy(q, 1 - core).wait_send()
    for c in range(stages):
        grad_keep(c).wait()
        for k in range(1, n):
            head_copy(k, c, me).wait_send()
            grad_copy(k, c, me).wait_send()
            grad_copy(k, c, lax.rem(me + n - k, n)).wait_recv()


def body(qkv_input, latents, cotangent, out_weight, gate_table, timesteps, frames):
    tok, wide = latents.shape
    n, n_dp = lax.axis_size("seq"), lax.axis_size("dp")
    rows = tok * n
    span, cols = out_weight.shape
    stages = 3
    n_chips = n_dp // 2
    turned = cols % HD != 0
    bf16 = jnp.bfloat16
    vmem = pl.BlockSpec(memory_space=pltpu.VMEM)
    smem = pl.BlockSpec(memory_space=pltpu.SMEM)
    dma = pltpu.SemaphoreType.DMA
    output, grads, grad_weight = pl.pallas_call(
        functools.partial(sublayer_kernel, n, n_dp, stages),
        out_shape=(
            jax.ShapeDtypeStruct((tok, wide), bf16),
            jax.ShapeDtypeStruct((3, tok, wide), bf16),
            jax.ShapeDtypeStruct((cols, span) if turned else (span, cols), jnp.float32),
        ),
        in_specs=[vmem, vmem, vmem, vmem, vmem, smem, smem],
        out_specs=(vmem, vmem, vmem),
        scratch_shapes=[
            pltpu.VMEM((3, rows, span), bf16),
            pltpu.VMEM((rows, span), bf16),
            pltpu.VMEM((rows, wide), bf16),
            pltpu.VMEM((wide, span), bf16),
            pltpu.VMEM((wide, span), bf16),
            pltpu.VMEM((n_chips, cols, span), bf16),
            pltpu.VMEM((n_chips - 1, cols, span), bf16),
            pltpu.VMEM((rows, wide), bf16),
            pltpu.VMEM((2, n, tok, wide), bf16),
            pltpu.VMEM((rows, span), bf16),
            pltpu.VMEM((3, rows, span), bf16),
            dma,
            dma((stages,)),
            dma((n - 1, stages)),
            dma((n - 1, stages)),
            dma((2, n)),
            dma((2, n)),
            dma((n_chips - 1,)),
            dma((n_chips - 1,)),
            dma((n_chips,)),
            dma((n_chips,)),
            dma((2, n)),
            dma((2, n)),
            dma((n - 1, stages)),
            dma((n - 1, stages)),
            dma((n_chips,)),
            dma((n_chips,)),
            dma((n_chips - 1,)),
            dma((n_chips - 1,)),
        ],
        compiler_params=pltpu.CompilerParams(
            collective_id=0, has_side_effects=True, vmem_limit_bytes=60 * 2**20
        ),
        cost_estimate=pl.CostEstimate(
            flops=30 * rows * wide * span, bytes_accessed=32 * 2**20, transcendentals=0
        ),
        name="sublayer",
    )(
        qkv_input.transpose(1, 0, 2), latents, cotangent,
        out_weight.T if turned else out_weight, gate_table, timesteps, frames,
    )
    return output, grads.transpose(1, 0, 2), grad_weight.T if turned else grad_weight


def solution(mesh):
    placed = (
        P(("dp", "seq"), None, None),
        P(("dp", "seq"), None),
        P(("dp", "seq"), None),
        P("seq", "dp"),
        P(),
        P("dp", None),
        P("dp", None),
    )
    return jax.shard_map(
        body,
        mesh=mesh,
        in_specs=placed,
        out_specs=(P(("dp", "seq"), None), P(("dp", "seq"), None, None), P("seq", "dp")),
        check_vma=False,
    )
```

```python
import functools

import jax
import jax.numpy as jnp
from jax import lax
from jax.experimental import pallas as pl
from jax.experimental.pallas import tpu as pltpu
from jax.sharding import PartitionSpec as P

HD = 128
FRAME_TOK = 64
QUERY_TILE = 256
MESH = pl.DeviceIdType.MESH
TRANSPOSED_RHS = (((1,), (1,)), ((), ()))
TRANSPOSED_LHS = (((0,), (0,)), ((), ()))


def dot(a, b, dims=(((1,), (0,)), ((), ()))):
    return lax.dot_general(a, b, dims, preferred_element_type=jnp.float32)


def greet(devices):
    barrier = pltpu.get_barrier_semaphore()
    for device in devices:
        pl.semaphore_signal(barrier, inc=1, device_id=device, device_id_type=MESH)
    pl.semaphore_wait(barrier, len(devices))


def clip_of(frames_ref, places):
    end = 0
    which = jnp.zeros_like(places)
    for c in range(frames_ref.shape[1] - 1):
        end = end + frames_ref[0, c] * FRAME_TOK
        which = which + (places >= end).astype(jnp.int32)
    return which


def gate_rows(table_ref, steps_ref, frames_ref, start, count):
    places = start + lax.broadcasted_iota(jnp.int32, (count, 1), 0)
    which = clip_of(frames_ref, places)
    gate = table_ref[pl.ds(steps_ref[0, 0], 1), :]
    for c in range(1, steps_ref.shape[1]):
        gate = jnp.where(which >= c, table_ref[pl.ds(steps_ref[0, c], 1), :], gate)
    return gate


def probabilities(q, k, frames_ref, start, rows):
    count = q.shape[0]
    scores = dot(q, k, TRANSPOSED_RHS) * jnp.float32(HD ** -0.5)
    mine = clip_of(frames_ref, start + lax.broadcasted_iota(jnp.int32, (count, 1), 0))
    theirs = clip_of(frames_ref, lax.broadcasted_iota(jnp.int32, (1, rows), 1))
    scores = jnp.where(mine == theirs, scores, jnp.float32(-1e30))
    expo = jnp.exp(scores - jnp.max(scores, axis=-1, keepdims=True))
    return expo * (1.0 / jnp.sum(expo, axis=-1, keepdims=True))


def sublayer_kernel(
    n, n_dp, stages,
    qkv_ref, lat_ref, cot_ref, w_ref, table_ref, steps_ref, frames_ref,
    out_ref, grads_ref, gw_ref,
    heads, attn, piece, weight, dweight, sibling, chips, part, landed, dattn, gbuf,
    own_sem, keep_sem, qs_sem, qr_sem, gs_sem, gr_sem,
    ws_sem, wr_sem, fs_sem, fr_sem, ps_sem, pr_sem, hs_sem, hr_sem,
    ss_sem, sr_sem, cs_sem, cr_sem,
):
    me = lax.axis_index("seq")
    dp = lax.axis_index("dp")
    core = lax.rem(dp, 2)
    chip = lax.div(dp, 2)
    n_chips = n_dp // 2
    rows, span = attn.shape
    tok, wide = out_ref.shape
    cols = wide // n_dp
    tile = min(QUERY_TILE, rows)
    chunk = span // stages
    step = 512

    def slab(block):
        return pl.ds(pl.multiple_of(block * tok, tok), tok)

    def owned(block):
        return pl.ds(pl.multiple_of(block * cols, cols), cols)

    def lanes(start):
        return pl.ds(pl.multiple_of(start, HD), chunk)

    def remote(src, dst, send, recv, device):
        return pltpu.make_async_remote_copy(
            src_ref=src, dst_ref=dst, send_sem=send, recv_sem=recv,
            device_id=device, device_id_type=MESH,
        )

    twin = (dp + 1 - 2 * core, me)

    def along(k):
        return (dp, lax.rem(me + k, n))

    def across(k):
        return (2 * lax.rem(chip + k, n_chips) + core, me)

    def block_copy(side, block):
        here = piece.at[slab(block), :]
        to = lax.rem(me + 1, n) if side == 0 else lax.rem(me + n - 1, n)
        return remote(here, here, gs_sem.at[side, block], gr_sem.at[side, block], (dp, to))

    def head_copy(k, c, source):
        peer = along(k)
        return remote(
            qkv_ref.at[:, :, lanes(peer[1] * span + c * chunk)],
            heads.at[:, slab(source), lanes(c * chunk)],
            qs_sem.at[k - 1, c], qr_sem.at[k - 1, c], peer,
        )

    def weight_copy(k):
        here = weight.at[owned(dp), :]
        return remote(
            here, here, ws_sem.at[k - 1], wr_sem.at[k - 1], across(k),
        )

    def weight_pass(k, source, side):
        here = weight.at[owned(2 * source + side), :]
        return remote(here, here, fs_sem.at[k], fr_sem.at[k], twin)

    def sum_copy(side, block):
        to = lax.rem(me + 1, n) if side == 0 else lax.rem(me + n - 1, n)
        return remote(
            part.at[slab(block), :], landed.at[side, block],
            ps_sem.at[side, block], pr_sem.at[side, block], (dp, to),
        )

    def grad_copy(k, c, source):
        peer = along(k)
        return remote(
            gbuf.at[:, slab(peer[1]), lanes(c * chunk)],
            grads_ref.at[:, :, lanes(source * span + c * chunk)],
            hs_sem.at[k - 1, c], hr_sem.at[k - 1, c], peer,
        )

    def grad_keep(c):
        return pltpu.make_async_copy(
            gbuf.at[:, slab(me), lanes(c * chunk)],
            grads_ref.at[:, :, lanes(me * span + c * chunk)], keep_sem.at[c],
        )

    def pair_copy(q, side):
        return remote(
            dweight.at[owned(2 * q + side), :], sibling.at[q],
            ss_sem.at[q], sr_sem.at[q], twin,
        )

    def chip_copy(k):
        return remote(
            dweight.at[owned(2 * lax.rem(chip + k, n_chips) + core), :], chips.at[k - 1],
            cs_sem.at[k - 1], cr_sem.at[k - 1], across(k),
        )

    greet(
        [along(k) for k in range(1, n)] + [across(k) for k in range(1, n_chips)] + [twin]
    )

    def send_heads(c):
        for k in range(1, n):
            head_copy(k, c, me).start()

    for c in range(stages):
        send_heads(c)
    own = pltpu.make_async_copy(
        qkv_ref.at[:, :, pl.ds(pl.multiple_of(me * span, span), span)],
        heads.at[:, slab(me), :], own_sem,
    )
    own.start()
    weight[owned(dp), :] = w_ref[...].T if w_ref.shape[0] == span else w_ref[...]
    for k in range(1, n_chips):
        weight_copy(k).start()
    weight_pass(0, chip, core).start()
    gate = gate_rows(table_ref, steps_ref, frames_ref, me * tok, tok)
    piece[slab(me), :] = (gate * cot_ref[...].astype(jnp.float32)).astype(jnp.bfloat16)
    own.wait()

    def start_gather():
        @pl.when(me < n - 1)
        def _():
            block_copy(0, me).start()

        @pl.when(me > 0)
        def _():
            block_copy(1, me).start()

    def heads_landed(c):
        for k in range(1, n):
            head_copy(k, c, lax.rem(me + n - k, n)).wait_recv()

    def forward(c):
        @pl.loop(0, (chunk // HD) * (rows // tile))
        def _(i):
            t, h = lax.rem(i, rows // tile), lax.div(i, rows // tile)
            here = pl.ds(pl.multiple_of(t * tile, tile), tile)
            head = pl.ds(pl.multiple_of(c * chunk + h * HD, HD), HD)
            probs = probabilities(
                heads[0, here, head], heads[1, :, head], frames_ref, t * tile, rows
            )
            mixed = dot(probs.astype(jnp.bfloat16), heads[2, :, head])
            attn[here, head] = mixed.astype(jnp.bfloat16)

    def backward(c):
        @pl.loop(0, chunk // HD)
        def _(h):
            head = pl.ds(pl.multiple_of(c * chunk + h * HD, HD), HD)
            grad_k = jnp.zeros((rows, HD), jnp.float32)
            grad_v = jnp.zeros((rows, HD), jnp.float32)
            for t in range(rows // tile):
                here = slice(t * tile, (t + 1) * tile)
                q, keys = heads[0, here, head], heads[1, :, head]
                probs = probabilities(q, keys, frames_ref, t * tile, rows)
                up = dattn[here, head]
                dprobs = dot(up, heads[2, :, head], TRANSPOSED_RHS)
                dprobs = dprobs.astype(jnp.bfloat16).astype(jnp.float32)
                dscores = probs * (dprobs - jnp.sum(probs * dprobs, axis=-1, keepdims=True))
                dscores = (dscores * jnp.float32(HD ** -0.5)).astype(jnp.bfloat16)
                gbuf[0, here, head] = dot(dscores, keys).astype(jnp.bfloat16)
                grad_k = grad_k + dot(dscores, q, TRANSPOSED_LHS)
                grad_v = grad_v + dot(probs.astype(jnp.bfloat16), up, TRANSPOSED_LHS)
            gbuf[1, :, head] = grad_k.astype(jnp.bfloat16)
            gbuf[2, :, head] = grad_v.astype(jnp.bfloat16)

        for k in range(1, n):
            grad_copy(k, c, me).start()
        grad_keep(c).start()

    def pull_back(block):
        dattn[slab(block), :] = dot(piece[slab(block), :], weight[...]).astype(jnp.bfloat16)

    def gather_hop(s):
        @pl.when(me - s >= 0)
        def _():
            block_copy(0, me - s).wait_recv()

            @pl.when(me < n - 1)
            def _():
                block_copy(0, me - s).start()

            pull_back(me - s)

        @pl.when(me + s < n)
        def _():
            block_copy(1, me + s).wait_recv()

            @pl.when(me > 0)
            def _():
                block_copy(1, me + s).start()

            pull_back(me + s)

    heads_landed(0)
    start_gather()
    forward(0)
    for k in range(1, n_chips):
        source = lax.rem(chip + n_chips - k, n_chips)
        weight_copy(k).wait_recv()
        weight_pass(k, source, core).start()
    for c in range(1, stages):
        heads_landed(c)
        forward(c)
    for k in range(n_chips):
        weight_pass(k, lax.rem(chip + n_chips - k, n_chips), 1 - core).wait_recv()

    @pl.loop(0, wide // step)
    def _(i):
        here = pl.ds(pl.multiple_of(i * step, step), step)
        part[:, here] = dot(attn[...], weight[here, :], TRANSPOSED_RHS).astype(jnp.bfloat16)

    for s in range(n - 1, 0, -1):
        @pl.when((me == 0) & (me + s < n))
        def _():
            sum_copy(0, me + s).start()

        @pl.when((me == n - 1) & (me - s >= 0))
        def _():
            sum_copy(1, me - s).start()

    def add_into(target, spot, other, count):
        @pl.loop(0, count // 16)
        def _(r):
            mine = pl.ds(pl.multiple_of(spot * count + r * 16, 16), 16)
            theirs = pl.ds(pl.multiple_of(r * 16, 16), 16)
            target[mine, :] = (
                target[mine, :].astype(jnp.float32) + other[theirs, :].astype(jnp.float32)
            ).astype(jnp.bfloat16)

    def relay(side, block):
        sum_copy(side, block).wait_recv()
        add_into(part, block, landed.at[side, block], tok)
        sum_copy(side, block).start()

    def relay_right(s):
        @pl.when((n - s > me) & (me > 0))
        def _():
            relay(0, n - s)

    def relay_left(s):
        @pl.when((s - 1 < me) & (me < n - 1))
        def _():
            relay(1, s - 1)

    def relays(near, far):
        @pl.when(2 * me < n)
        def _():
            for s in near:
                relay_right(s)
            for s in far:
                relay_left(s)

        @pl.when(2 * me >= n)
        def _():
            for s in near:
                relay_left(s)
            for s in far:
                relay_right(s)

    def stage_hops(c):
        return range(1 + c * (n - 1) // stages, 1 + (c + 1) * (n - 1) // stages)

    pull_back(me)
    for s in range(1, n):
        gather_hop(s)
    relays(stage_hops(0), ())
    for c in range(stages):
        backward(c)
        if c == stages - 2:
            @pl.loop(0, wide // step)
            def _(i):
                here = pl.ds(pl.multiple_of(i * step, step), step)
                grown = dot(piece[:, here], attn[...], TRANSPOSED_LHS)
                dweight[here, :] = grown.astype(jnp.bfloat16)

            for q in range(n_chips):
                pair_copy(q, 1 - core).start()
        if c == stages - 1:
            for k in range(1, n_chips):
                q = lax.rem(chip + k, n_chips)
                pair_copy(q, core).wait_recv()
                add_into(dweight, 2 * q + core, sibling.at[q], cols)
                chip_copy(k).start()
        relays(stage_hops(c + 1) if c + 1 < stages else (), stage_hops(c))

    pair_copy(chip, core).wait_recv()
    total = dweight[owned(dp), :].astype(jnp.float32) + sibling[chip].astype(jnp.float32)
    for k in range(1, n_chips):
        chip_copy(k).wait_recv()
        total = total + chips[k - 1].astype(jnp.float32)
    gw_ref[...] = total.T if gw_ref.shape[0] == span else total

    @pl.when(me > 0)
    def _():
        sum_copy(0, me).wait_recv()

    @pl.when(me == 0)
    def _():
        landed[0, 0] = jnp.zeros_like(landed[0, 0])

    @pl.when(me < n - 1)
    def _():
        sum_copy(1, me).wait_recv()

    @pl.when(me == n - 1)
    def _():
        landed[1, n - 1] = jnp.zeros_like(landed[1, n - 1])

    gate = gate_rows(table_ref, steps_ref, frames_ref, me * tok, tok)
    proj = (
        part[slab(me), :].astype(jnp.float32)
        + landed[0, me].astype(jnp.float32)
        + landed[1, me].astype(jnp.float32)
    )
    out_ref[...] = (lat_ref[...].astype(jnp.float32) + gate * proj).astype(jnp.bfloat16)

    for s in range(n):
        @pl.when((me - s >= 0) & (me < n - 1))
        def _():
            block_copy(0, me - s).wait_send()

        @pl.when((me + s < n) & (me > 0))
        def _():
            block_copy(1, me + s).wait_send()

        if s > 0:
            @pl.when(me + s < n)
            def _():
                sum_copy(0, me + s).wait_send()

            @pl.when(me - s >= 0)
            def _():
                sum_copy(1, me - s).wait_send()

    for k in range(1, n_chips):
        weight_copy(k).wait_send()
        chip_copy(k).wait_send()
    for q in range(n_chips):
        weight_pass(q, lax.rem(chip + n_chips - q, n_chips), core).wait_send()
        pair_copy(q, 1 - core).wait_send()
    for c in range(stages):
        grad_keep(c).wait()
        for k in range(1, n):
            head_copy(k, c, me).wait_send()
            grad_copy(k, c, me).wait_send()
            grad_copy(k, c, lax.rem(me + n - k, n)).wait_recv()


def body(qkv_input, latents, cotangent, out_weight, gate_table, timesteps, frames):
    tok, wide = latents.shape
    n, n_dp = lax.axis_size("seq"), lax.axis_size("dp")
    rows = tok * n
    span, cols = out_weight.shape
    stages = 3
    n_chips = n_dp // 2
    turned = cols % HD != 0
    bf16 = jnp.bfloat16
    vmem = pl.BlockSpec(memory_space=pltpu.VMEM)
    smem = pl.BlockSpec(memory_space=pltpu.SMEM)
    dma = pltpu.SemaphoreType.DMA
    output, grads, grad_weight = pl.pallas_call(
        functools.partial(sublayer_kernel, n, n_dp, stages),
        out_shape=(
            jax.ShapeDtypeStruct((tok, wide), bf16),
            jax.ShapeDtypeStruct((3, tok, wide), bf16),
            jax.ShapeDtypeStruct((cols, span) if turned else (span, cols), jnp.float32),
        ),
        in_specs=[vmem, vmem, vmem, vmem, vmem, smem, smem],
        out_specs=(vmem, vmem, vmem),
        scratch_shapes=[
            pltpu.VMEM((3, rows, span), bf16),
            pltpu.VMEM((rows, span), bf16),
            pltpu.VMEM((rows, wide), bf16),
            pltpu.VMEM((wide, span), bf16),
            pltpu.VMEM((wide, span), bf16),
            pltpu.VMEM((n_chips, cols, span), bf16),
            pltpu.VMEM((n_chips - 1, cols, span), bf16),
            pltpu.VMEM((rows, wide), bf16),
            pltpu.VMEM((2, n, tok, wide), bf16),
            pltpu.VMEM((rows, span), bf16),
            pltpu.VMEM((3, rows, span), bf16),
            dma,
            dma((stages,)),
            dma((n - 1, stages)),
            dma((n - 1, stages)),
            dma((2, n)),
            dma((2, n)),
            dma((n_chips - 1,)),
            dma((n_chips - 1,)),
            dma((n_chips,)),
            dma((n_chips,)),
            dma((2, n)),
            dma((2, n)),
            dma((n - 1, stages)),
            dma((n - 1, stages)),
            dma((n_chips,)),
            dma((n_chips,)),
            dma((n_chips - 1,)),
            dma((n_chips - 1,)),
        ],
        compiler_params=pltpu.CompilerParams(
            collective_id=0, has_side_effects=True, vmem_limit_bytes=60 * 2**20
        ),
        cost_estimate=pl.CostEstimate(
            flops=30 * rows * wide * span, bytes_accessed=32 * 2**20, transcendentals=0
        ),
        name="sublayer",
    )(
        qkv_input.transpose(1, 0, 2), latents, cotangent,
        out_weight.T if turned else out_weight, gate_table, timesteps, frames,
    )
    return output, grads.transpose(1, 0, 2), grad_weight.T if turned else grad_weight


def solution(mesh):
    placed = (
        P(("dp", "seq"), None, None),
        P(("dp", "seq"), None),
        P(("dp", "seq"), None),
        P("seq", "dp"),
        P(),
        P("dp", None),
        P("dp", None),
    )
    return jax.shard_map(
        body,
        mesh=mesh,
        in_specs=placed,
        out_specs=(P(("dp", "seq"), None), P(("dp", "seq"), None, None), P("seq", "dp")),
        check_vma=False,
    )
```

```python
import functools

import jax
import jax.numpy as jnp
from jax import lax
from jax.experimental import pallas as pl
from jax.experimental.pallas import tpu as pltpu
from jax.sharding import PartitionSpec as P

HD = 128
FRAME_TOK = 64
QUERY_TILE = 256
MESH = pl.DeviceIdType.MESH
TRANSPOSED_RHS = (((1,), (1,)), ((), ()))
TRANSPOSED_LHS = (((0,), (0,)), ((), ()))


def dot(a, b, dims=(((1,), (0,)), ((), ()))):
    return lax.dot_general(a, b, dims, preferred_element_type=jnp.float32)


def greet(devices):
    barrier = pltpu.get_barrier_semaphore()
    for device in devices:
        pl.semaphore_signal(barrier, inc=1, device_id=device, device_id_type=MESH)
    pl.semaphore_wait(barrier, len(devices))


def clip_of(frames_ref, places):
    end = 0
    which = jnp.zeros_like(places)
    for c in range(frames_ref.shape[1] - 1):
        end = end + frames_ref[0, c] * FRAME_TOK
        which = which + (places >= end).astype(jnp.int32)
    return which


def gate_rows(table_ref, steps_ref, frames_ref, start, count):
    places = start + lax.broadcasted_iota(jnp.int32, (count, 1), 0)
    which = clip_of(frames_ref, places)
    gate = table_ref[pl.ds(steps_ref[0, 0], 1), :]
    for c in range(1, steps_ref.shape[1]):
        gate = jnp.where(which >= c, table_ref[pl.ds(steps_ref[0, c], 1), :], gate)
    return gate


def probabilities(q, k, frames_ref, start, rows):
    count = q.shape[0]
    scores = dot(q, k, TRANSPOSED_RHS) * jnp.float32(HD ** -0.5)
    mine = clip_of(frames_ref, start + lax.broadcasted_iota(jnp.int32, (count, 1), 0))
    theirs = clip_of(frames_ref, lax.broadcasted_iota(jnp.int32, (1, rows), 1))
    scores = jnp.where(mine == theirs, scores, jnp.float32(-1e30))
    expo = jnp.exp(scores - jnp.max(scores, axis=-1, keepdims=True))
    return expo * (1.0 / jnp.sum(expo, axis=-1, keepdims=True))


def sublayer_kernel(
    n, n_dp, stages,
    qkv_ref, lat_ref, cot_ref, w_ref, table_ref, steps_ref, frames_ref,
    out_ref, grads_ref, gw_ref,
    heads, attn, piece, weight, dweight, sibling, chips, part, landed, dattn, gbuf,
    own_sem, keep_sem, qs_sem, qr_sem, gs_sem, gr_sem,
    ws_sem, wr_sem, fs_sem, fr_sem, ps_sem, pr_sem, hs_sem, hr_sem,
    ss_sem, sr_sem, cs_sem, cr_sem,
):
    me = lax.axis_index("seq")
    dp = lax.axis_index("dp")
    core = lax.rem(dp, 2)
    chip = lax.div(dp, 2)
    n_chips = n_dp // 2
    rows, span = attn.shape
    tok, wide = out_ref.shape
    cols = wide // n_dp
    tile = min(QUERY_TILE, rows)
    chunk = span // stages
    step = 512

    def slab(block):
        return pl.ds(pl.multiple_of(block * tok, tok), tok)

    def owned(block):
        return pl.ds(pl.multiple_of(block * cols, cols), cols)

    def lanes(start):
        return pl.ds(pl.multiple_of(start, HD), chunk)

    def remote(src, dst, send, recv, device):
        return pltpu.make_async_remote_copy(
            src_ref=src, dst_ref=dst, send_sem=send, recv_sem=recv,
            device_id=device, device_id_type=MESH,
        )

    twin = (dp + 1 - 2 * core, me)

    def along(k):
        return (dp, lax.rem(me + k, n))

    def across(k):
        return (2 * lax.rem(chip + k, n_chips) + core, me)

    def block_copy(side, block):
        here = piece.at[slab(block), :]
        to = lax.rem(me + 1, n) if side == 0 else lax.rem(me + n - 1, n)
        return remote(here, here, gs_sem.at[side, block], gr_sem.at[side, block], (dp, to))

    def head_copy(k, c, source):
        peer = along(k)
        return remote(
            qkv_ref.at[:, :, lanes(peer[1] * span + c * chunk)],
            heads.at[:, slab(source), lanes(c * chunk)],
            qs_sem.at[k - 1, c], qr_sem.at[k - 1, c], peer,
        )

    def weight_copy(k):
        here = weight.at[owned(dp), :]
        return remote(
            here, here, ws_sem.at[k - 1], wr_sem.at[k - 1], across(k),
        )

    def weight_pass(k, source, side):
        here = weight.at[owned(2 * source + side), :]
        return remote(here, here, fs_sem.at[k], fr_sem.at[k], twin)

    def sum_copy(side, block):
        to = lax.rem(me + 1, n) if side == 0 else lax.rem(me + n - 1, n)
        return remote(
            part.at[slab(block), :], landed.at[side, block],
            ps_sem.at[side, block], pr_sem.at[side, block], (dp, to),
        )

    def grad_copy(k, c, source):
        peer = along(k)
        return remote(
            gbuf.at[:, slab(peer[1]), lanes(c * chunk)],
            grads_ref.at[:, :, lanes(source * span + c * chunk)],
            hs_sem.at[k - 1, c], hr_sem.at[k - 1, c], peer,
        )

    def grad_keep(c):
        return pltpu.make_async_copy(
            gbuf.at[:, slab(me), lanes(c * chunk)],
            grads_ref.at[:, :, lanes(me * span + c * chunk)], keep_sem.at[c],
        )

    def pair_copy(q, side):
        return remote(
            dweight.at[owned(2 * q + side), :], sibling.at[q],
            ss_sem.at[q], sr_sem.at[q], twin,
        )

    def chip_copy(k):
        return remote(
            dweight.at[owned(2 * lax.rem(chip + k, n_chips) + core), :], chips.at[k - 1],
            cs_sem.at[k - 1], cr_sem.at[k - 1], across(k),
        )

    greet(
        [along(k) for k in range(1, n)] + [across(k) for k in range(1, n_chips)] + [twin]
    )

    def send_heads(c):
        for k in range(1, n):
            head_copy(k, c, me).start()

    for c in range(stages):
        send_heads(c)
    own = pltpu.make_async_copy(
        qkv_ref.at[:, :, pl.ds(pl.multiple_of(me * span, span), span)],
        heads.at[:, slab(me), :], own_sem,
    )
    own.start()
    weight[owned(dp), :] = w_ref[...].T if w_ref.shape[0] == span else w_ref[...]
    for k in range(1, n_chips):
        weight_copy(k).start()
    weight_pass(0, chip, core).start()
    gate = gate_rows(table_ref, steps_ref, frames_ref, me * tok, tok)
    piece[slab(me), :] = (gate * cot_ref[...].astype(jnp.float32)).astype(jnp.bfloat16)
    own.wait()

    def start_gather():
        @pl.when(me < n - 1)
        def _():
            block_copy(0, me).start()

        @pl.when(me > 0)
        def _():
            block_copy(1, me).start()

    def heads_landed(c):
        for k in range(1, n):
            head_copy(k, c, lax.rem(me + n - k, n)).wait_recv()

    def forward(c):
        @pl.loop(0, (chunk // HD) * (rows // tile))
        def _(i):
            t, h = lax.rem(i, rows // tile), lax.div(i, rows // tile)
            here = pl.ds(pl.multiple_of(t * tile, tile), tile)
            head = pl.ds(pl.multiple_of(c * chunk + h * HD, HD), HD)
            probs = probabilities(
                heads[0, here, head], heads[1, :, head], frames_ref, t * tile, rows
            )
            mixed = dot(probs.astype(jnp.bfloat16), heads[2, :, head])
            attn[here, head] = mixed.astype(jnp.bfloat16)

    def backward(c):
        @pl.loop(0, chunk // HD)
        def _(h):
            head = pl.ds(pl.multiple_of(c * chunk + h * HD, HD), HD)
            grad_k = jnp.zeros((rows, HD), jnp.float32)
            grad_v = jnp.zeros((rows, HD), jnp.float32)
            for t in range(rows // tile):
                here = slice(t * tile, (t + 1) * tile)
                q, keys = heads[0, here, head], heads[1, :, head]
                probs = probabilities(q, keys, frames_ref, t * tile, rows)
                up = dattn[here, head]
                dprobs = dot(up, heads[2, :, head], TRANSPOSED_RHS)
                dprobs = dprobs.astype(jnp.bfloat16).astype(jnp.float32)
                dscores = probs * (dprobs - jnp.sum(probs * dprobs, axis=-1, keepdims=True))
                dscores = (dscores * jnp.float32(HD ** -0.5)).astype(jnp.bfloat16)
                gbuf[0, here, head] = dot(dscores, keys).astype(jnp.bfloat16)
                grad_k = grad_k + dot(dscores, q, TRANSPOSED_LHS)
                grad_v = grad_v + dot(probs.astype(jnp.bfloat16), up, TRANSPOSED_LHS)
            gbuf[1, :, head] = grad_k.astype(jnp.bfloat16)
            gbuf[2, :, head] = grad_v.astype(jnp.bfloat16)

        for k in range(1, n):
            grad_copy(k, c, me).start()
        grad_keep(c).start()

    def pull_back(block):
        dattn[slab(block), :] = dot(piece[slab(block), :], weight[...]).astype(jnp.bfloat16)

    def gather_hop(s):
        @pl.when(me - s >= 0)
        def _():
            block_copy(0, me - s).wait_recv()

            @pl.when(me < n - 1)
            def _():
                block_copy(0, me - s).start()

            pull_back(me - s)

        @pl.when(me + s < n)
        def _():
            block_copy(1, me + s).wait_recv()

            @pl.when(me > 0)
            def _():
                block_copy(1, me + s).start()

            pull_back(me + s)

    heads_landed(0)
    start_gather()
    forward(0)
    for k in range(1, n_chips):
        source = lax.rem(chip + n_chips - k, n_chips)
        weight_copy(k).wait_recv()
        weight_pass(k, source, core).start()
    for c in range(1, stages):
        heads_landed(c)
        forward(c)
    for k in range(n_chips):
        weight_pass(k, lax.rem(chip + n_chips - k, n_chips), 1 - core).wait_recv()

    @pl.loop(0, wide // step)
    def _(i):
        here = pl.ds(pl.multiple_of(i * step, step), step)
        part[:, here] = dot(attn[...], weight[here, :], TRANSPOSED_RHS).astype(jnp.bfloat16)

    for s in range(n - 1, 0, -1):
        @pl.when((me == 0) & (me + s < n))
        def _():
            sum_copy(0, me + s).start()

        @pl.when((me == n - 1) & (me - s >= 0))
        def _():
            sum_copy(1, me - s).start()

    def add_into(target, spot, other, count):
        @pl.loop(0, count // 16)
        def _(r):
            mine = pl.ds(pl.multiple_of(spot * count + r * 16, 16), 16)
            theirs = pl.ds(pl.multiple_of(r * 16, 16), 16)
            target[mine, :] = (
                target[mine, :].astype(jnp.float32) + other[theirs, :].astype(jnp.float32)
            ).astype(jnp.bfloat16)

    def relay(side, block):
        sum_copy(side, block).wait_recv()
        add_into(part, block, landed.at[side, block], tok)
        sum_copy(side, block).start()

    def relay_right(s):
        @pl.when((n - s > me) & (me > 0))
        def _():
            relay(0, n - s)

    def relay_left(s):
        @pl.when((s - 1 < me) & (me < n - 1))
        def _():
            relay(1, s - 1)

    def relays(near, far):
        @pl.when(2 * me < n)
        def _():
            for s in near:
                relay_right(s)
            for s in far:
                relay_left(s)

        @pl.when(2 * me >= n)
        def _():
            for s in near:
                relay_left(s)
            for s in far:
                relay_right(s)

    def stage_hops(c):
        return range(1 + c * (n - 1) // stages, 1 + (c + 1) * (n - 1) // stages)

    pull_back(me)
    for s in range(1, n):
        gather_hop(s)
        if s == 1:
            relays(stage_hops(0), ())
    for c in range(stages):
        backward(c)
        if c == stages - 2:
            @pl.loop(0, wide // step)
            def _(i):
                here = pl.ds(pl.multiple_of(i * step, step), step)
                grown = dot(piece[:, here], attn[...], TRANSPOSED_LHS)
                dweight[here, :] = grown.astype(jnp.bfloat16)

            for q in range(n_chips):
                pair_copy(q, 1 - core).start()
        if c == stages - 1:
            for k in range(1, n_chips):
                q = lax.rem(chip + k, n_chips)
                pair_copy(q, core).wait_recv()
                add_into(dweight, 2 * q + core, sibling.at[q], cols)
                chip_copy(k).start()
        relays(stage_hops(c + 1) if c + 1 < stages else (), stage_hops(c))

    pair_copy(chip, core).wait_recv()
    total = dweight[owned(dp), :].astype(jnp.float32) + sibling[chip].astype(jnp.float32)
    for k in range(1, n_chips):
        chip_copy(k).wait_recv()
        total = total + chips[k - 1].astype(jnp.float32)
    gw_ref[...] = total.T if gw_ref.shape[0] == span else total

    @pl.when(me > 0)
    def _():
        sum_copy(0, me).wait_recv()

    @pl.when(me == 0)
    def _():
        landed[0, 0] = jnp.zeros_like(landed[0, 0])

    @pl.when(me < n - 1)
    def _():
        sum_copy(1, me).wait_recv()

    @pl.when(me == n - 1)
    def _():
        landed[1, n - 1] = jnp.zeros_like(landed[1, n - 1])

    gate = gate_rows(table_ref, steps_ref, frames_ref, me * tok, tok)
    proj = (
        part[slab(me), :].astype(jnp.float32)
        + landed[0, me].astype(jnp.float32)
        + landed[1, me].astype(jnp.float32)
    )
    out_ref[...] = (lat_ref[...].astype(jnp.float32) + gate * proj).astype(jnp.bfloat16)

    for s in range(n):
        @pl.when((me - s >= 0) & (me < n - 1))
        def _():
            block_copy(0, me - s).wait_send()

        @pl.when((me + s < n) & (me > 0))
        def _():
            block_copy(1, me + s).wait_send()

        if s > 0:
            @pl.when(me + s < n)
            def _():
                sum_copy(0, me + s).wait_send()

            @pl.when(me - s >= 0)
            def _():
                sum_copy(1, me - s).wait_send()

    for k in range(1, n_chips):
        weight_copy(k).wait_send()
        chip_copy(k).wait_send()
    for q in range(n_chips):
        weight_pass(q, lax.rem(chip + n_chips - q, n_chips), core).wait_send()
        pair_copy(q, 1 - core).wait_send()
    for c in range(stages):
        grad_keep(c).wait()
        for k in range(1, n):
            head_copy(k, c, me).wait_send()
            grad_copy(k, c, me).wait_send()
            grad_copy(k, c, lax.rem(me + n - k, n)).wait_recv()


def body(qkv_input, latents, cotangent, out_weight, gate_table, timesteps, frames):
    tok, wide = latents.shape
    n, n_dp = lax.axis_size("seq"), lax.axis_size("dp")
    rows = tok * n
    span, cols = out_weight.shape
    stages = 3
    n_chips = n_dp // 2
    turned = cols % HD != 0
    bf16 = jnp.bfloat16
    vmem = pl.BlockSpec(memory_space=pltpu.VMEM)
    smem = pl.BlockSpec(memory_space=pltpu.SMEM)
    anyspace = pl.BlockSpec(memory_space=pl.ANY)
    dma = pltpu.SemaphoreType.DMA
    output, grads, grad_weight = pl.pallas_call(
        functools.partial(sublayer_kernel, n, n_dp, stages),
        out_shape=(
            jax.ShapeDtypeStruct((tok, wide), bf16),
            jax.ShapeDtypeStruct((3, tok, wide), bf16),
            jax.ShapeDtypeStruct((cols, span) if turned else (span, cols), jnp.float32),
        ),
        in_specs=[anyspace, vmem, vmem, vmem, vmem, smem, smem],
        out_specs=(vmem, anyspace, vmem),
        scratch_shapes=[
            pltpu.VMEM((3, rows, span), bf16),
            pltpu.VMEM((rows, span), bf16),
            pltpu.VMEM((rows, wide), bf16),
            pltpu.VMEM((wide, span), bf16),
            pltpu.VMEM((wide, span), bf16),
            pltpu.VMEM((n_chips, cols, span), bf16),
            pltpu.VMEM((n_chips - 1, cols, span), bf16),
            pltpu.VMEM((rows, wide), bf16),
            pltpu.VMEM((2, n, tok, wide), bf16),
            pltpu.VMEM((rows, span), bf16),
            pltpu.VMEM((3, rows, span), bf16),
            dma,
            dma((stages,)),
            dma((n - 1, stages)),
            dma((n - 1, stages)),
            dma((2, n)),
            dma((2, n)),
            dma((n_chips - 1,)),
            dma((n_chips - 1,)),
            dma((n_chips,)),
            dma((n_chips,)),
            dma((2, n)),
            dma((2, n)),
            dma((n - 1, stages)),
            dma((n - 1, stages)),
            dma((n_chips,)),
            dma((n_chips,)),
            dma((n_chips - 1,)),
            dma((n_chips - 1,)),
        ],
        compiler_params=pltpu.CompilerParams(
            collective_id=0, has_side_effects=True, vmem_limit_bytes=60 * 2**20
        ),
        cost_estimate=pl.CostEstimate(
            flops=30 * rows * wide * span, bytes_accessed=32 * 2**20, transcendentals=0
        ),
        name="sublayer",
    )(
        qkv_input.transpose(1, 0, 2), latents, cotangent,
        out_weight.T if turned else out_weight, gate_table, timesteps, frames,
    )
    return output, grads.transpose(1, 0, 2), grad_weight.T if turned else grad_weight


def solution(mesh):
    placed = (
        P(("dp", "seq"), None, None),
        P(("dp", "seq"), None),
        P(("dp", "seq"), None),
        P("seq", "dp"),
        P(),
        P("dp", None),
        P("dp", None),
    )
    return jax.shard_map(
        body,
        mesh=mesh,
        in_specs=placed,
        out_specs=(P(("dp", "seq"), None), P(("dp", "seq"), None, None), P("seq", "dp")),
        check_vma=False,
    )
```

```python
import functools

import jax
import jax.numpy as jnp
from jax import lax
from jax.experimental import pallas as pl
from jax.experimental.pallas import tpu as pltpu
from jax.sharding import PartitionSpec as P

HD = 128
FRAME_TOK = 64
QUERY_TILE = 256
MESH = pl.DeviceIdType.MESH
TRANSPOSED_RHS = (((1,), (1,)), ((), ()))
TRANSPOSED_LHS = (((0,), (0,)), ((), ()))


def dot(a, b, dims=(((1,), (0,)), ((), ()))):
    return lax.dot_general(a, b, dims, preferred_element_type=jnp.float32)


def greet(devices):
    barrier = pltpu.get_barrier_semaphore()
    for device in devices:
        pl.semaphore_signal(barrier, inc=1, device_id=device, device_id_type=MESH)
    pl.semaphore_wait(barrier, len(devices))


def clip_of(frames_ref, places):
    end = 0
    which = jnp.zeros_like(places)
    for c in range(frames_ref.shape[1] - 1):
        end = end + frames_ref[0, c] * FRAME_TOK
        which = which + (places >= end).astype(jnp.int32)
    return which


def gate_rows(table_ref, steps_ref, frames_ref, start, count):
    places = start + lax.broadcasted_iota(jnp.int32, (count, 1), 0)
    which = clip_of(frames_ref, places)
    gate = table_ref[pl.ds(steps_ref[0, 0], 1), :]
    for c in range(1, steps_ref.shape[1]):
        gate = jnp.where(which >= c, table_ref[pl.ds(steps_ref[0, c], 1), :], gate)
    return gate


def probabilities(q, k, frames_ref, start, rows):
    count = q.shape[0]
    scores = dot(q, k, TRANSPOSED_RHS) * jnp.float32(HD ** -0.5)
    mine = clip_of(frames_ref, start + lax.broadcasted_iota(jnp.int32, (count, 1), 0))
    theirs = clip_of(frames_ref, lax.broadcasted_iota(jnp.int32, (1, rows), 1))
    scores = jnp.where(mine == theirs, scores, jnp.float32(-1e30))
    expo = jnp.exp(scores - jnp.max(scores, axis=-1, keepdims=True))
    return expo * (1.0 / jnp.sum(expo, axis=-1, keepdims=True))


def sublayer_kernel(
    n, n_dp, stages,
    qkv_ref, lat_ref, cot_ref, w_ref, table_ref, steps_ref, frames_ref,
    out_ref, grads_ref, gw_ref,
    heads, attn, piece, weight, dweight, sibling, chips, part, landed, dattn, gbuf,
    own_sem, keep_sem, qs_sem, qr_sem, gs_sem, gr_sem,
    ws_sem, wr_sem, fs_sem, fr_sem, ps_sem, pr_sem, hs_sem, hr_sem,
    ss_sem, sr_sem, cs_sem, cr_sem,
):
    me = lax.axis_index("seq")
    dp = lax.axis_index("dp")
    core = lax.rem(dp, 2)
    chip = lax.div(dp, 2)
    n_chips = n_dp // 2
    rows, span = attn.shape
    tok, wide = out_ref.shape
    cols = wide // n_dp
    tile = min(QUERY_TILE, rows)
    chunk = span // stages
    step = 512

    def slab(block):
        return pl.ds(pl.multiple_of(block * tok, tok), tok)

    def owned(block):
        return pl.ds(pl.multiple_of(block * cols, cols), cols)

    def lanes(start):
        return pl.ds(pl.multiple_of(start, HD), chunk)

    def remote(src, dst, send, recv, device):
        return pltpu.make_async_remote_copy(
            src_ref=src, dst_ref=dst, send_sem=send, recv_sem=recv,
            device_id=device, device_id_type=MESH,
        )

    twin = (dp + 1 - 2 * core, me)

    def along(k):
        return (dp, lax.rem(me + k, n))

    def across(k):
        return (2 * lax.rem(chip + k, n_chips) + core, me)

    def block_copy(side, block):
        here = piece.at[slab(block), :]
        to = lax.rem(me + 1, n) if side == 0 else lax.rem(me + n - 1, n)
        return remote(here, here, gs_sem.at[side, block], gr_sem.at[side, block], (dp, to))

    def head_copy(k, c, source):
        peer = along(k)
        return remote(
            qkv_ref.at[:, :, lanes(peer[1] * span + c * chunk)],
            heads.at[:, slab(source), lanes(c * chunk)],
            qs_sem.at[k - 1, c], qr_sem.at[k - 1, c], peer,
        )

    def weight_copy(k):
        here = weight.at[owned(dp), :]
        return remote(
            here, here, ws_sem.at[k - 1], wr_sem.at[k - 1], across(k),
        )

    def weight_pass(k, source, side):
        here = weight.at[owned(2 * source + side), :]
        return remote(here, here, fs_sem.at[k], fr_sem.at[k], twin)

    def sum_copy(side, block):
        to = lax.rem(me + 1, n) if side == 0 else lax.rem(me + n - 1, n)
        return remote(
            part.at[slab(block), :], landed.at[side, block],
            ps_sem.at[side, block], pr_sem.at[side, block], (dp, to),
        )

    def grad_copy(k, c, source):
        peer = along(k)
        return remote(
            gbuf.at[:, slab(peer[1]), lanes(c * chunk)],
            grads_ref.at[:, :, lanes(source * span + c * chunk)],
            hs_sem.at[k - 1, c], hr_sem.at[k - 1, c], peer,
        )

    def grad_keep(c):
        return pltpu.make_async_copy(
            gbuf.at[:, slab(me), lanes(c * chunk)],
            grads_ref.at[:, :, lanes(me * span + c * chunk)], keep_sem.at[c],
        )

    def pair_copy(q, side):
        return remote(
            dweight.at[owned(2 * q + side), :], sibling.at[q],
            ss_sem.at[q], sr_sem.at[q], twin,
        )

    def chip_copy(k):
        return remote(
            dweight.at[owned(2 * lax.rem(chip + k, n_chips) + core), :], chips.at[k - 1],
            cs_sem.at[k - 1], cr_sem.at[k - 1], across(k),
        )

    greet(
        [along(k) for k in range(1, n)] + [across(k) for k in range(1, n_chips)] + [twin]
    )

    def send_heads(c):
        for k in range(1, n):
            head_copy(k, c, me).start()

    for c in range(stages):
        send_heads(c)
    own = pltpu.make_async_copy(
        qkv_ref.at[:, :, pl.ds(pl.multiple_of(me * span, span), span)],
        heads.at[:, slab(me), :], own_sem,
    )
    own.start()
    weight[owned(dp), :] = w_ref[...].T if w_ref.shape[0] == span else w_ref[...]
    for k in range(1, n_chips):
        weight_copy(k).start()
    weight_pass(0, chip, core).start()
    gate = gate_rows(table_ref, steps_ref, frames_ref, me * tok, tok)
    piece[slab(me), :] = (gate * cot_ref[...].astype(jnp.float32)).astype(jnp.bfloat16)
    own.wait()

    def start_gather():
        @pl.when(me < n - 1)
        def _():
            block_copy(0, me).start()

        @pl.when(me > 0)
        def _():
            block_copy(1, me).start()

    def heads_landed(c):
        for k in range(1, n):
            head_copy(k, c, lax.rem(me + n - k, n)).wait_recv()

    def forward(c):
        @pl.loop(0, (chunk // HD) * (rows // tile))
        def _(i):
            t, h = lax.rem(i, rows // tile), lax.div(i, rows // tile)
            here = pl.ds(pl.multiple_of(t * tile, tile), tile)
            head = pl.ds(pl.multiple_of(c * chunk + h * HD, HD), HD)
            probs = probabilities(
                heads[0, here, head], heads[1, :, head], frames_ref, t * tile, rows
            )
            mixed = dot(probs.astype(jnp.bfloat16), heads[2, :, head])
            attn[here, head] = mixed.astype(jnp.bfloat16)

    def backward(c):
        @pl.loop(0, chunk // HD)
        def _(h):
            head = pl.ds(pl.multiple_of(c * chunk + h * HD, HD), HD)
            grad_k = jnp.zeros((rows, HD), jnp.float32)
            grad_v = jnp.zeros((rows, HD), jnp.float32)
            for t in range(rows // tile):
                here = slice(t * tile, (t + 1) * tile)
                q, keys = heads[0, here, head], heads[1, :, head]
                probs = probabilities(q, keys, frames_ref, t * tile, rows)
                up = dattn[here, head]
                dprobs = dot(up, heads[2, :, head], TRANSPOSED_RHS)
                dprobs = dprobs.astype(jnp.bfloat16).astype(jnp.float32)
                dscores = probs * (dprobs - jnp.sum(probs * dprobs, axis=-1, keepdims=True))
                dscores = (dscores * jnp.float32(HD ** -0.5)).astype(jnp.bfloat16)
                gbuf[0, here, head] = dot(dscores, keys).astype(jnp.bfloat16)
                grad_k = grad_k + dot(dscores, q, TRANSPOSED_LHS)
                grad_v = grad_v + dot(probs.astype(jnp.bfloat16), up, TRANSPOSED_LHS)
            gbuf[1, :, head] = grad_k.astype(jnp.bfloat16)
            gbuf[2, :, head] = grad_v.astype(jnp.bfloat16)

        for k in range(1, n):
            grad_copy(k, c, me).start()
        grad_keep(c).start()

    def pull_back(block):
        dattn[slab(block), :] = dot(piece[slab(block), :], weight[...]).astype(jnp.bfloat16)

    def gather_hop(s):
        @pl.when(me - s >= 0)
        def _():
            block_copy(0, me - s).wait_recv()

            @pl.when(me < n - 1)
            def _():
                block_copy(0, me - s).start()

            pull_back(me - s)

        @pl.when(me + s < n)
        def _():
            block_copy(1, me + s).wait_recv()

            @pl.when(me > 0)
            def _():
                block_copy(1, me + s).start()

            pull_back(me + s)

    heads_landed(0)
    start_gather()
    forward(0)
    for k in range(1, n_chips):
        source = lax.rem(chip + n_chips - k, n_chips)
        weight_copy(k).wait_recv()
        weight_pass(k, source, core).start()
    for c in range(1, stages):
        heads_landed(c)
        forward(c)
    for k in range(n_chips):
        weight_pass(k, lax.rem(chip + n_chips - k, n_chips), 1 - core).wait_recv()

    @pl.loop(0, wide // step)
    def _(i):
        here = pl.ds(pl.multiple_of(i * step, step), step)
        part[:, here] = dot(attn[...], weight[here, :], TRANSPOSED_RHS).astype(jnp.bfloat16)

    for s in range(n - 1, 0, -1):
        @pl.when((me == 0) & (me + s < n))
        def _():
            sum_copy(0, me + s).start()

        @pl.when((me == n - 1) & (me - s >= 0))
        def _():
            sum_copy(1, me - s).start()

    def add_into(target, spot, other, count):
        @pl.loop(0, count // 16)
        def _(r):
            mine = pl.ds(pl.multiple_of(spot * count + r * 16, 16), 16)
            theirs = pl.ds(pl.multiple_of(r * 16, 16), 16)
            target[mine, :] = (
                target[mine, :].astype(jnp.float32) + other[theirs, :].astype(jnp.float32)
            ).astype(jnp.bfloat16)

    def relay(side, block):
        sum_copy(side, block).wait_recv()
        add_into(part, block, landed.at[side, block], tok)
        sum_copy(side, block).start()

    def relay_right(s):
        @pl.when((n - s > me) & (me > 0))
        def _():
            relay(0, n - s)

    def relay_left(s):
        @pl.when((s - 1 < me) & (me < n - 1))
        def _():
            relay(1, s - 1)

    def relays(near, far):
        @pl.when(2 * me < n)
        def _():
            for s in near:
                relay_right(s)
            for s in far:
                relay_left(s)

        @pl.when(2 * me >= n)
        def _():
            for s in near:
                relay_left(s)
            for s in far:
                relay_right(s)

    def stage_hops(c):
        return range(1 + c * (n - 1) // stages, 1 + (c + 1) * (n - 1) // stages)

    pull_back(me)
    for s in range(1, n):
        gather_hop(s)
        if s == 1:
            relays(stage_hops(0), ())
    for c in range(stages):
        backward(c)
        if c == stages - 2:
            @pl.loop(0, wide // step)
            def _(i):
                here = pl.ds(pl.multiple_of(i * step, step), step)
                grown = dot(piece[:, here], attn[...], TRANSPOSED_LHS)
                dweight[here, :] = grown.astype(jnp.bfloat16)

            for q in range(n_chips):
                pair_copy(q, 1 - core).start()
        if c == stages - 1:
            for k in range(1, n_chips):
                q = lax.rem(chip + k, n_chips)
                pair_copy(q, core).wait_recv()
                add_into(dweight, 2 * q + core, sibling.at[q], cols)
                chip_copy(k).start()
        relays(stage_hops(c + 1) if c + 1 < stages else (), stage_hops(c))

    pair_copy(chip, core).wait_recv()
    total = dweight[owned(dp), :].astype(jnp.float32) + sibling[chip].astype(jnp.float32)
    for k in range(1, n_chips):
        chip_copy(k).wait_recv()
        total = total + chips[k - 1].astype(jnp.float32)
    gw_ref[...] = total.T if gw_ref.shape[0] == span else total

    @pl.when(me > 0)
    def _():
        sum_copy(0, me).wait_recv()

    @pl.when(me == 0)
    def _():
        landed[0, 0] = jnp.zeros_like(landed[0, 0])

    @pl.when(me < n - 1)
    def _():
        sum_copy(1, me).wait_recv()

    @pl.when(me == n - 1)
    def _():
        landed[1, n - 1] = jnp.zeros_like(landed[1, n - 1])

    gate = gate_rows(table_ref, steps_ref, frames_ref, me * tok, tok)
    proj = (
        part[slab(me), :].astype(jnp.float32)
        + landed[0, me].astype(jnp.float32)
        + landed[1, me].astype(jnp.float32)
    )
    out_ref[...] = (lat_ref[...].astype(jnp.float32) + gate * proj).astype(jnp.bfloat16)

    for s in range(n):
        @pl.when((me - s >= 0) & (me < n - 1))
        def _():
            block_copy(0, me - s).wait_send()

        @pl.when((me + s < n) & (me > 0))
        def _():
            block_copy(1, me + s).wait_send()

        if s > 0:
            @pl.when(me + s < n)
            def _():
                sum_copy(0, me + s).wait_send()

            @pl.when(me - s >= 0)
            def _():
                sum_copy(1, me - s).wait_send()

    for k in range(1, n_chips):
        weight_copy(k).wait_send()
        chip_copy(k).wait_send()
    for q in range(n_chips):
        weight_pass(q, lax.rem(chip + n_chips - q, n_chips), core).wait_send()
        pair_copy(q, 1 - core).wait_send()
    for c in range(stages):
        grad_keep(c).wait()
        for k in range(1, n):
            head_copy(k, c, me).wait_send()
            grad_copy(k, c, me).wait_send()
            grad_copy(k, c, lax.rem(me + n - k, n)).wait_recv()


def store_kernel(out_in, grads_in, out_ref, grads_ref):
    out_ref[...] = out_in[...]
    grads_ref[...] = grads_in[...]


def body(qkv_input, latents, cotangent, out_weight, gate_table, timesteps, frames):
    tok, wide = latents.shape
    n, n_dp = lax.axis_size("seq"), lax.axis_size("dp")
    rows = tok * n
    span, cols = out_weight.shape
    stages = 3
    n_chips = n_dp // 2
    turned = cols % HD != 0
    bf16 = jnp.bfloat16
    vmem = pl.BlockSpec(memory_space=pltpu.VMEM)
    smem = pl.BlockSpec(memory_space=pltpu.SMEM)
    anyspace = pl.BlockSpec(memory_space=pl.ANY)
    dma = pltpu.SemaphoreType.DMA
    output, grads, grad_weight = pl.pallas_call(
        functools.partial(sublayer_kernel, n, n_dp, stages),
        out_shape=(
            jax.ShapeDtypeStruct((tok, wide), bf16),
            jax.ShapeDtypeStruct((3, tok, wide), bf16),
            jax.ShapeDtypeStruct((cols, span) if turned else (span, cols), jnp.float32),
        ),
        in_specs=[anyspace, vmem, vmem, vmem, vmem, smem, smem],
        out_specs=(vmem, anyspace, vmem),
        scratch_shapes=[
            pltpu.VMEM((3, rows, span), bf16),
            pltpu.VMEM((rows, span), bf16),
            pltpu.VMEM((rows, wide), bf16),
            pltpu.VMEM((wide, span), bf16),
            pltpu.VMEM((wide, span), bf16),
            pltpu.VMEM((n_chips, cols, span), bf16),
            pltpu.VMEM((n_chips - 1, cols, span), bf16),
            pltpu.VMEM((rows, wide), bf16),
            pltpu.VMEM((2, n, tok, wide), bf16),
            pltpu.VMEM((rows, span), bf16),
            pltpu.VMEM((3, rows, span), bf16),
            dma,
            dma((stages,)),
            dma((n - 1, stages)),
            dma((n - 1, stages)),
            dma((2, n)),
            dma((2, n)),
            dma((n_chips - 1,)),
            dma((n_chips - 1,)),
            dma((n_chips,)),
            dma((n_chips,)),
            dma((2, n)),
            dma((2, n)),
            dma((n - 1, stages)),
            dma((n - 1, stages)),
            dma((n_chips,)),
            dma((n_chips,)),
            dma((n_chips - 1,)),
            dma((n_chips - 1,)),
        ],
        compiler_params=pltpu.CompilerParams(
            collective_id=0, has_side_effects=True, vmem_limit_bytes=60 * 2**20
        ),
        cost_estimate=pl.CostEstimate(
            flops=30 * rows * wide * span, bytes_accessed=32 * 2**20, transcendentals=0
        ),
        name="sublayer",
    )(
        qkv_input.transpose(1, 0, 2), latents, cotangent,
        out_weight.T if turned else out_weight, gate_table, timesteps, frames,
    )
    share = tok // 4
    blocks = (
        pl.BlockSpec((share, wide), lambda i: (i, 0)),
        pl.BlockSpec((3, share, wide), lambda i: (0, i, 0)),
    )
    output, grads = pl.pallas_call(
        store_kernel,
        grid=(4,),
        out_shape=(
            jax.ShapeDtypeStruct(output.shape, bf16),
            jax.ShapeDtypeStruct(grads.shape, bf16),
        ),
        in_specs=blocks,
        out_specs=blocks,
        name="store",
    )(output, grads)
    return output, grads.transpose(1, 0, 2), grad_weight.T if turned else grad_weight


def solution(mesh):
    placed = (
        P(("dp", "seq"), None, None),
        P(("dp", "seq"), None),
        P(("dp", "seq"), None),
        P("seq", "dp"),
        P(),
        P("dp", None),
        P("dp", None),
    )
    return jax.shard_map(
        body,
        mesh=mesh,
        in_specs=placed,
        out_specs=(P(("dp", "seq"), None), P(("dp", "seq"), None, None), P("seq", "dp")),
        check_vma=False,
    )
```
